256 devices in a mesh: prompt: 16 (over z, x_hi), resp: 16 (over x_lo, y, core).
Axes of the slice: x: 4 (x_hi: 2, x_lo: 2; x = x_hi * 2 + x_lo), y: 4, z: 8, core: 2. Of those that a mesh axis runs over, the one named last changes fastest.
Arguments:
- queries: bfloat16 [32768, 8192], P(('prompt', 'resp')), may hold values from -24 to 24
- resp_keys: bfloat16 [32768, 1024], P(('prompt', 'resp')), may hold values from -4 to 4
- resp_values: bfloat16 [32768, 1024], P(('prompt', 'resp')), may hold values from -4 to 4
- prefix_keys: bfloat16 [16384, 1024], P(('prompt', 'resp')), may hold values from -16 to 16
- prefix_values: bfloat16 [16384, 1024], P(('prompt', 'resp')), may hold values from -4 to 4
- d_out: bfloat16 [32768, 8192], P(('prompt', 'resp')), may hold values from -6 to 6
- rewards: float32 [16, 16], P('prompt'), may hold values from -4 to 4
- prompt_len: int32 [16], P('prompt'), may hold values from 512 to 1024, as said below
- resp_len: int32 [16, 16], P('prompt'), may hold values from 1 to 128, as said below
- resp_assign: int32 [16, 16], P('prompt'), may hold values from 0 to 15, as said below
Outputs:
- attn_out: bfloat16 [32768, 8192], P(('prompt', 'resp'))
- d_queries: bfloat16 [32768, 8192], P(('prompt', 'resp'))
- d_resp_keys: bfloat16 [32768, 1024], P(('prompt', 'resp'))
- d_resp_values: bfloat16 [32768, 1024], P(('prompt', 'resp'))
- d_prefix_keys: bfloat16 [16384, 1024], P(('prompt', 'resp'))
- d_prefix_values: bfloat16 [16384, 1024], P(('prompt', 'resp'))
The draws below stay inside these ranges and needn't reach their ends.
Inputs may be any that keep to these rules, and one draw needn't show every extreme that they name: `resp_assign`: device d of a group holds exactly 1 of its responses. `resp_len`: the responses of one device add up to at most 128 tokens, and to exactly 128 on some device of every group. `prompt_len`: exactly 1024 in at least one group.
All inputs are finite; a program needn't handle non-finite values.
Results may differ from the reference program's by a relative error of at most 0.0085.
The reference program's roundings to bfloat16 on the way (of `cotangent`, `attention_bf` and `d_scores`) count: a program that leaves them out, or rounds other values in their place, can miss the bound.
Values may be sent and summed in bfloat16 or wider, within the bound.
No kernel may reach another device: no remote copies, remote signals or barrier semaphores. Data moves between devices by JAX's collectives and lax.ppermute only.
A program may use at most 192 MiB of HBM per device.

```python
import jax
import jax.numpy as jnp
from jax import lax

HEADS = 64
KV_HEADS = 8
HEAD_DIM = 128
GROUP_SIZE = 16
RESP_DEV = 128
PREFIX = 1024
GROUPS = 16
SPREAD = 16
ROWS = 32768
PROMPT_ROWS = 16384


def layout_draw(key):
    per_dev = GROUP_SIZE // SPREAD

    def one_group(group_key):
        key_order, key_fill, key_full, key_split = jax.random.split(group_key, 4)
        shuffled = jax.random.permutation(key_order, GROUP_SIZE)
        assign = (shuffled // per_dev).astype(jnp.int32)
        dev_fill = jax.random.randint(key_fill, (SPREAD,), RESP_DEV // 4, RESP_DEV + 1)
        full_dev = jax.random.randint(key_full, (), 0, SPREAD)
        dev_fill = jnp.where(jnp.arange(SPREAD) == full_dev, RESP_DEV, dev_fill)
        fill_of = dev_fill[assign]
        raw_len = 1 + jax.random.randint(key_split, (GROUP_SIZE,), 0, fill_of // per_dev)
        raw_len = jnp.where(assign == full_dev, 1, raw_len)
        resp_ids = jnp.arange(GROUP_SIZE)
        same_dev = assign[None, :] == assign[:, None]
        after_mine = same_dev & (resp_ids[None, :] > resp_ids[:, None])
        is_last = jnp.logical_not(jnp.any(after_mine, axis=1))
        others = jnp.sum(jnp.where(same_dev & (resp_ids[None, :] != resp_ids[:, None]), raw_len[None, :], 0), axis=1)
        lengths = jnp.where(is_last, fill_of - others, raw_len)
        return (assign, lengths.astype(jnp.int32))
    return jax.vmap(one_group)(jax.random.split(key, GROUPS))


def base_prefix(key):
    return jnp.clip(jax.random.normal(key, (PROMPT_ROWS, KV_HEADS * HEAD_DIM), jnp.float32), -4.0, 4.0)


def draw_resp_assign(key, part):
    assign, lengths = layout_draw(key)
    return assign


def draw_resp_len(key, part):
    assign, lengths = layout_draw(key)
    return lengths


def draw_prompt_len(key, part):
    key = jax.random.fold_in(key, 3)
    key_len, key_full = jax.random.split(key)
    drawn_len = jax.random.randint(key_len, (GROUPS,), PREFIX // 2, PREFIX + 1)
    full_group = jax.random.randint(key_full, (), 0, GROUPS)
    return jnp.where(jnp.arange(GROUPS) == full_group, PREFIX, drawn_len).astype(jnp.int32)


def draw_prefix_keys(key, part):
    keys_base = base_prefix(key)
    return keys_base.astype(jnp.bfloat16)


def draw_queries(key, part):
    key = jax.random.fold_in(key, 7)
    width = HEADS * HEAD_DIM
    values = jnp.clip(jax.random.normal(key, (ROWS, width), jnp.float32), -4.0, 4.0)
    return values.astype(jnp.bfloat16)


def level_of(key, shape, pieces, smallest, top_value):
    def one(dim, parts):
        heights = jax.random.uniform(jax.random.fold_in(jax.random.fold_in(key, 6), dim), (parts,), jnp.float32, smallest / len(pieces), top_value / len(pieces))
        return jnp.repeat(jnp.exp(heights), shape[dim] // parts).reshape((-1,) + (1,) * (len(shape) - dim - 1))

    factor_of = one(*pieces[0])
    for cut in pieces[1:]:
        factor_of = factor_of * one(*cut)
    return factor_of


def centred(rng, extent, spread, reach, cuts=(), kind=jnp.bfloat16):
    loudness = level_of(rng, extent, cuts, -0.22, 0.18) if cuts else 1.0
    array = jax.random.normal(rng, extent, jnp.float32) * spread * loudness
    return jnp.minimum(jnp.maximum(array, -reach), reach).astype(kind)


def setup_inputs(seed: int = 0) -> dict:
    seeds = jax.random.split(jax.random.key(seed), 11)
    queries = draw_queries(jax.random.fold_in(seeds[10], 71), 0)
    resp_keys = centred(seeds[1], (ROWS, KV_HEADS * HEAD_DIM), 1.0, 4.0, ((0, 256),))
    resp_values = centred(seeds[2], (ROWS, KV_HEADS * HEAD_DIM), 1.0, 4.0, ((0, 256),))
    prefix_keys = draw_prefix_keys(jax.random.fold_in(seeds[10], 71), 0)
    prefix_values = centred(seeds[4], (PROMPT_ROWS, KV_HEADS * HEAD_DIM), 1.0, 4.0, ((0, 256),))
    d_out = centred(seeds[5], (ROWS, HEADS * HEAD_DIM), 1.0, 6.0, ((0, 256),))
    rewards = centred(seeds[6], (GROUPS, GROUP_SIZE), 1.0, 4.0, ((0, 16),), jnp.float32)
    prompt_len = draw_prompt_len(jax.random.fold_in(seeds[10], 71), 0)
    resp_len = draw_resp_len(jax.random.fold_in(seeds[10], 71), 0)
    resp_assign = draw_resp_assign(jax.random.fold_in(seeds[10], 71), 0)
    return dict(queries=queries, resp_keys=resp_keys, resp_values=resp_values, prefix_keys=prefix_keys, prefix_values=prefix_values, d_out=d_out, rewards=rewards, prompt_len=prompt_len, resp_len=resp_len, resp_assign=resp_assign)


def slot_layout(lengths, assign, device, slot_count):
    on_device = assign == device
    used_len = jnp.where(on_device, lengths, 0)
    start_at = jnp.cumsum(used_len) - used_len
    slot_ids = lax.broadcasted_iota(jnp.int32, (slot_count, lengths.shape[0]), 0)
    inside = on_device[None, :] & (slot_ids >= start_at[None, :]) & (slot_ids < (start_at + used_len)[None, :])
    member = inside.astype(jnp.float32)
    live_slot = jnp.sum(member, axis=1)
    return inside, member, live_slot


def allowed_keys(inside, prompt_end, prefix_rows):
    slot_count = inside.shape[0]
    same_resp = jnp.any(inside[:, None, :] & inside[None, :, :], axis=2)
    query_ids = lax.broadcasted_iota(jnp.int32, (slot_count, slot_count), 0)
    key_ids = lax.broadcasted_iota(jnp.int32, (slot_count, slot_count), 1)
    resp_ok = same_resp & (key_ids <= query_ids)
    prefix_ok = lax.broadcasted_iota(jnp.int32, (slot_count, prefix_rows), 1) < prompt_end
    return jnp.concatenate([prefix_ok, resp_ok], axis=1)


def product(form, left, right):
    return jnp.einsum(form, left.astype(jnp.float32), right.astype(jnp.float32), precision=lax.Precision.HIGHEST)


def attend(queries, resp_keys, resp_values, keys_pre, values_pre, cotangent, allowed, live_slot):
    slot_count = queries.shape[0]
    per_kv = HEADS // KV_HEADS
    query_four = queries.reshape(slot_count, KV_HEADS, per_kv, HEAD_DIM)
    cot_four = cotangent.reshape(slot_count, KV_HEADS, per_kv, HEAD_DIM)
    keys_all = jnp.concatenate([keys_pre, resp_keys], axis=0).reshape(-1, KV_HEADS, HEAD_DIM)
    values_all = jnp.concatenate([values_pre, resp_values], axis=0).reshape(-1, KV_HEADS, HEAD_DIM)
    scale_qk = HEAD_DIM ** -0.5

    def one_group(group_index):
        group_q = lax.dynamic_index_in_dim(query_four, group_index, 1, keepdims=False)
        group_cot = lax.dynamic_index_in_dim(cot_four, group_index, 1, keepdims=False)
        group_k = lax.dynamic_index_in_dim(keys_all, group_index, 1, keepdims=False)
        group_v = lax.dynamic_index_in_dim(values_all, group_index, 1, keepdims=False)
        scores = product("rqd,kd->qrk", group_q, group_k) * scale_qk
        scores = jnp.where(allowed[None], scores, -jnp.inf)
        row_max = jnp.max(scores, axis=2, keepdims=True)
        exp_scores = jnp.where(allowed[None], jnp.exp(scores - row_max), 0.0)
        row_sum = jnp.sum(exp_scores, axis=2, keepdims=True)
        attention = exp_scores / row_sum
        attention_bf = attention.astype(jnp.bfloat16)
        out_f = product("qrk,kd->rqd", attention_bf, group_v)
        out_bf = (out_f * live_slot[:, None, None]).astype(jnp.bfloat16)
        row_dot = jnp.sum(group_cot.astype(jnp.float32) * out_bf.astype(jnp.float32), axis=2)
        d_probs = product("rqd,kd->qrk", group_cot, group_v)
        d_scores = (attention * (d_probs - jnp.transpose(row_dot)[:, :, None])).astype(jnp.bfloat16)
        d_query = (product("qrk,kd->rqd", d_scores, group_k) * scale_qk).astype(jnp.bfloat16)
        d_keys = product("qrk,rqd->kd", d_scores, group_q) * scale_qk
        d_values = product("qrk,rqd->kd", attention_bf, group_cot)
        return out_bf, d_query, d_keys, d_values

    out_all, dq_all, dk_all, dv_all = lax.map(one_group, jnp.arange(KV_HEADS, dtype=jnp.int32))
    out_all = jnp.transpose(out_all, (1, 0, 2, 3)).reshape(slot_count, HEADS * HEAD_DIM)
    dq_all = jnp.transpose(dq_all, (1, 0, 2, 3)).reshape(slot_count, HEADS * HEAD_DIM)
    dk_all = jnp.transpose(dk_all, (1, 0, 2)).reshape(-1, KV_HEADS * HEAD_DIM)
    dv_all = jnp.transpose(dv_all, (1, 0, 2)).reshape(-1, KV_HEADS * HEAD_DIM)
    prefix_rows = keys_pre.shape[0]
    return out_all, dq_all, dk_all[prefix_rows:], dv_all[prefix_rows:], dk_all[:prefix_rows], dv_all[:prefix_rows]


def reference(queries, resp_keys, resp_values, prefix_keys, prefix_values, d_out, rewards, prompt_len, resp_len, resp_assign):
    live_total = jnp.sum(resp_len).astype(jnp.float32)
    grad_scale = (GROUPS * SPREAD * RESP_DEV) / live_total
    kv_width = KV_HEADS * HEAD_DIM

    def per_group(group_id):
        keys_pre = lax.dynamic_slice_in_dim(prefix_keys, group_id * PREFIX, PREFIX, 0)
        values_pre = lax.dynamic_slice_in_dim(prefix_values, group_id * PREFIX, PREFIX, 0)
        reward_row = lax.dynamic_index_in_dim(rewards, group_id, 0, keepdims=False)
        advantage = reward_row - jnp.mean(reward_row)
        lengths = lax.dynamic_index_in_dim(resp_len, group_id, 0, keepdims=False)
        assign = lax.dynamic_index_in_dim(resp_assign, group_id, 0, keepdims=False)
        prompt_end = lax.dynamic_index_in_dim(prompt_len, group_id, 0, keepdims=False)

        def per_device(carry, device):
            row_start = (group_id * SPREAD + device) * RESP_DEV
            block_q = lax.dynamic_slice_in_dim(queries, row_start, RESP_DEV, 0)
            block_k = lax.dynamic_slice_in_dim(resp_keys, row_start, RESP_DEV, 0)
            block_v = lax.dynamic_slice_in_dim(resp_values, row_start, RESP_DEV, 0)
            block_d = lax.dynamic_slice_in_dim(d_out, row_start, RESP_DEV, 0)
            inside, member, live_slot = slot_layout(lengths, assign, device, RESP_DEV)
            weight = -grad_scale * jnp.sum(member * advantage[None, :], axis=1)
            cotangent = (block_d.astype(jnp.float32) * weight[:, None]).astype(jnp.bfloat16)
            allowed = allowed_keys(inside, prompt_end, PREFIX)
            results = attend(block_q, block_k, block_v, keys_pre, values_pre, cotangent, allowed, live_slot)
            grads = jnp.concatenate([results[4], results[5]], axis=1)
            return carry + grads, (results[0], results[1], results[2], results[3])

        zero_grads = jnp.zeros((PREFIX, 2 * kv_width), jnp.float32)
        summed, blocks = lax.scan(per_device, zero_grads, jnp.arange(SPREAD, dtype=jnp.int32))
        return blocks, summed

    blocks, summed = lax.map(per_group, jnp.arange(GROUPS, dtype=jnp.int32))
    attn_out = blocks[0].reshape(ROWS, HEADS * HEAD_DIM)
    d_queries = blocks[1].reshape(ROWS, HEADS * HEAD_DIM)
    d_resp_keys = blocks[2].reshape(ROWS, kv_width).astype(jnp.bfloat16)
    d_resp_values = blocks[3].reshape(ROWS, kv_width).astype(jnp.bfloat16)
    d_prefix_keys = summed[:, :, :kv_width].reshape(PROMPT_ROWS, kv_width).astype(jnp.bfloat16)
    d_prefix_values = summed[:, :, kv_width:].reshape(PROMPT_ROWS, kv_width).astype(jnp.bfloat16)
    return (attn_out, d_queries, d_resp_keys, d_resp_values, d_prefix_keys, d_prefix_values)
```

```python
import functools

import jax
import jax.numpy as jnp
from jax import lax
from jax.experimental import pallas as pl
from jax.experimental.pallas import tpu as pltpu
from jax.sharding import PartitionSpec as P

HEADS = 64
KV_HEADS = 8
HEAD_DIM = 128
PER_KV = HEADS // KV_HEADS
LOCAL = KV_HEADS // 2
SLOTS = 128
OWN = 64
PREFIX = 1024
KEYS = PREFIX + SLOTS
WIDE = PER_KV * HEAD_DIM
PACK = 2 * WIDE + 2 * HEAD_DIM
TILE = 512
SCALE = HEAD_DIM**-0.5
SCALE2 = SCALE * 1.4426950408889634
SPREAD = 16
GROUPS = 16
PARTS = ((0, 1), (2, 3))

BF = jnp.bfloat16
F32 = jnp.float32
NT = (((1,), (1,)), ((), ()))
NN = (((1,), (0,)), ((), ()))
ANY = pl.BlockSpec(memory_space=pl.ANY)
SMEM = pl.BlockSpec(memory_space=pltpu.SMEM)


def dot(a, b, dims):
    return lax.dot_general(a, b, dims, preferred_element_type=F32)


def shape(*dims, dtype=BF):
    return jax.ShapeDtypeStruct(dims, dtype)


def pack_prompt_kernel(heads, k_ref, v_ref, out):
    for n, h in enumerate(heads):
        for core in range(2):
            cols = slice((core * LOCAL + h) * HEAD_DIM, (core * LOCAL + h + 1) * HEAD_DIM)
            k = k_ref[:, cols]
            v = v_ref[:, cols]
            for chip in range(SPREAD // 2):
                out[2 * chip + core, :, 2 * n * HEAD_DIM : (2 * n + 1) * HEAD_DIM] = k
                out[2 * chip + core, :, (2 * n + 1) * HEAD_DIM : (2 * n + 2) * HEAD_DIM] = v


def pack_prompt(heads, keys, values):
    return pl.pallas_call(
        functools.partial(pack_prompt_kernel, heads),
        out_shape=shape(SPREAD, OWN, len(heads) * 2 * HEAD_DIM),
        name="pack_prompt",
    )(keys, values)


def unpack_rows_kernel(place, packed, *refs):
    out, dq, dk, dv = refs[-4:]
    out[...] = packed[:, :WIDE]
    dq[...] = packed[:, WIDE : 2 * WIDE]
    dk[...] = packed[:, 2 * WIDE : 2 * WIDE + HEAD_DIM]
    dv[...] = packed[:, 2 * WIDE + HEAD_DIM :]


def unpack_rows(place, packed, heads, bufs):
    theirs = lambda h, place: (0, (1 - place[1]) * LOCAL + heads[0] + h)
    wide = pl.BlockSpec((SLOTS, WIDE), theirs)
    narrow = pl.BlockSpec((SLOTS, HEAD_DIM), theirs)
    return pl.pallas_call(
        unpack_rows_kernel,
        grid_spec=pltpu.PrefetchScalarGridSpec(
            num_scalar_prefetch=1,
            grid=(len(heads),),
            in_specs=[pl.BlockSpec((SLOTS, PACK), lambda h, place: (0, h))] + [ANY] * 4,
            out_specs=[wide, wide, narrow, narrow],
        ),
        out_shape=[shape(SLOTS, HEADS * HEAD_DIM)] * 2 + [shape(SLOTS, KV_HEADS * HEAD_DIM)] * 2,
        input_output_aliases={2 + i: i for i in range(4)},
        name="unpack_rows",
    )(place, packed, *bufs)


def sum_terms_kernel(heads, terms, *refs):
    dk_ref, dv_ref = refs[-2:]
    if len(refs) > 2:
        dk_ref[...] = refs[0][...]
        dv_ref[...] = refs[1][...]
    for n, h in enumerate(heads):
        cols = slice(2 * n * HEAD_DIM, (2 * n + 2) * HEAD_DIM)
        for core in range(2):
            total = terms[core, :, cols].astype(F32)
            for chip in range(1, SPREAD // 2):
                total = total + terms[2 * chip + core, :, cols].astype(F32)
            total = total.astype(BF)
            own = slice((core * LOCAL + h) * HEAD_DIM, (core * LOCAL + h + 1) * HEAD_DIM)
            dk_ref[:, own] = total[:, :HEAD_DIM]
            dv_ref[:, own] = total[:, HEAD_DIM:]


def sum_terms(heads, terms, bufs):
    return pl.pallas_call(
        functools.partial(sum_terms_kernel, heads),
        out_shape=[shape(OWN, KV_HEADS * HEAD_DIM)] * 2,
        name="sum_terms",
    )(terms, *bufs)


def head_kernel(n_alias, place, prompt_len, resp_len, resp_assign, rewards, *refs):
    totals = refs[:4]
    q_ref, do_ref, kr_ref, vr_ref, q2_ref, do2_ref, kr2_ref, vr2_ref, kv_ref = refs[4:13]
    out_ref, dq_ref, dkr_ref, dvr_ref, back, grads = refs[13 + n_alias : 19 + n_alias]
    bias, weight, live, ks, vs, qs, cs, dka, dva = refs[19 + n_alias :]

    @pl.when(pl.program_id(0) == 0)
    def _():
        key = lax.broadcasted_iota(jnp.int32, (SLOTS, PREFIX), 1)
        row = lax.broadcasted_iota(jnp.int32, (SLOTS, SLOTS), 0)
        col = lax.broadcasted_iota(jnp.int32, (SLOTS, SLOTS), 1)
        resp_bias = jnp.where(col <= row, 0.0, -jnp.inf)
        bias[:, :SLOTS] = resp_bias
        bias[:, SLOTS:KEYS] = jnp.where(key < prompt_len[0], 0.0, -jnp.inf)
        bias[:, KEYS:] = resp_bias
        mean = rewards[0, 0]
        for i in range(1, SPREAD):
            mean = mean + rewards[0, i]
        mean = mean * (1.0 / SPREAD)
        live_total = jnp.sum((totals[0][...] + totals[1][...] + totals[2][...] + totals[3][...]).astype(F32))
        grad_scale = jnp.full((SLOTS, SLOTS), 1.0 * GROUPS * SPREAD * SLOTS, F32) / live_total
        for b in range(2):
            device = place[0] if b == 0 else place[0] + 1 - 2 * place[1]
            length = 0
            advantage = 0.0
            for i in range(SPREAD):
                here = resp_assign[0, i] == device
                length = length + jnp.where(here, resp_len[0, i], 0)
                advantage = advantage + jnp.where(here, rewards[0, i] - mean, 0.0)
            alive = jnp.where(row < length, 1.0, 0.0)
            live[b] = alive
            weight[b] = -grad_scale * (advantage * alive)

    ks[:SLOTS, :] = kr_ref[...]
    ks[SLOTS:KEYS, :] = kv_ref[:, :HEAD_DIM]
    ks[KEYS:, :] = kr2_ref[...]
    vs[:SLOTS, :] = vr_ref[...]
    vs[SLOTS:KEYS, :] = kv_ref[:, HEAD_DIM:]
    vs[KEYS:, :] = vr2_ref[...]
    for b, (q, do) in enumerate(((q_ref, do_ref), (q2_ref, do2_ref))):
        w = weight[b]
        for j in range(PER_KV):
            cols = slice(j * HEAD_DIM, (j + 1) * HEAD_DIM)
            rows = slice(j * SLOTS, (j + 1) * SLOTS)
            qs[b, rows, :] = q[:, cols]
            cs[b, rows, :] = (do[:, cols].astype(F32) * w).astype(BF)

    per = TILE // SLOTS
    tiles = PER_KV * SLOTS // TILE
    units = [(b, t) for b in range(2) for t in range(tiles)]
    spans = (slice(0, KEYS), slice(SLOTS, SLOTS + KEYS))

    def store(b, t, value, own, start):
        for i in range(per):
            j = t * per + i
            piece = value[i * SLOTS : (i + 1) * SLOTS]
            if b == 0:
                own[:, j * HEAD_DIM : (j + 1) * HEAD_DIM] = piece
            else:
                back[:, start + j * HEAD_DIM : start + (j + 1) * HEAD_DIM] = piece

    def softmax_part(b, t):
        rows = slice(t * TILE, (t + 1) * TILE)
        s = dot(qs[b, rows, :], ks[spans[b], :], NT)
        s = s + jnp.concatenate([bias[:, spans[b]]] * per, axis=0)
        m = jnp.max(s, axis=1, keepdims=True)
        p = jnp.exp2(s * SCALE2 - m * SCALE2)
        return p, 1.0 / jnp.sum(p, axis=1, keepdims=True)

    def score_part(b, t, p, inv):
        rows = slice(t * TILE, (t + 1) * TILE)
        c = cs[b, rows, :]
        att = p * inv
        ab = att.astype(BF)
        alive = jnp.concatenate([live[b]] * per, axis=0)
        ob = (dot(ab, vs[spans[b], :], NN) * alive).astype(BF)
        row_dot = jnp.sum(c.astype(F32) * ob.astype(F32), axis=1, keepdims=True)
        dp = dot(c, vs[spans[b], :], NT)
        ds = (att * (dp - row_dot)).astype(BF)
        store(b, t, ob, out_ref, 0)
        return ab, ds

    def grad_part(b, t, ab, ds):
        rows = slice(t * TILE, (t + 1) * TILE)
        store(b, t, (dot(ds, ks[spans[b], :], NN) * SCALE).astype(BF), dq_ref, WIDE)
        dv = dot(cs[b, rows, :].T, ab, NN)
        dk = dot(qs[b, rows, :].T, ds, NN)
        if t > 0:
            dv = dv + dva[b]
            dk = dk + dka[b]
        dva[b] = dv
        dka[b] = dk

    now = softmax_part(*units[0])
    last = None
    for u, unit in enumerate(units):
        later = softmax_part(*units[u + 1]) if u + 1 < len(units) else None
        if last is not None:
            grad_part(*units[u - 1], *last)
        last = score_part(*unit, *now)
        now = later
    grad_part(*units[-1], *last)

    dkr_ref[...] = (dka[0, :, :SLOTS] * SCALE).T.astype(BF)
    dvr_ref[...] = dva[0, :, :SLOTS].T.astype(BF)
    back[:, 2 * WIDE : 2 * WIDE + HEAD_DIM] = (dka[1, :, PREFIX:] * SCALE).T.astype(BF)
    back[:, 2 * WIDE + HEAD_DIM :] = dva[1, :, PREFIX:].T.astype(BF)
    grads[:, :HEAD_DIM] = ((dka[0, :, SLOTS:] + dka[1, :, :PREFIX]) * SCALE).T.astype(BF)
    grads[:, HEAD_DIM:] = (dva[0, :, SLOTS:] + dva[1, :, :PREFIX]).T.astype(BF)


def head_pass(scalars, totals, arrays, others, kv, heads, bufs):
    mine = lambda g, place: (0, place[1] * LOCAL + heads[0] + g)
    at = lambda g, place: (0, g)
    wide = pl.BlockSpec((SLOTS, WIDE), mine)
    narrow = pl.BlockSpec((SLOTS, HEAD_DIM), mine)
    total = pl.BlockSpec((1, SPREAD), lambda g, place: (0, 0))
    inputs = (*scalars, *totals, *arrays, *others, kv)
    n = len(heads)
    return pl.pallas_call(
        functools.partial(head_kernel, len(bufs)),
        grid_spec=pltpu.PrefetchScalarGridSpec(
            num_scalar_prefetch=1,
            grid=(n,),
            in_specs=[SMEM] * 4
            + [total] * 4
            + [wide, wide, narrow, narrow] * 2
            + [pl.BlockSpec((PREFIX, 2 * HEAD_DIM), at)]
            + [ANY] * len(bufs),
            out_specs=[
                wide,
                wide,
                narrow,
                narrow,
                pl.BlockSpec((SLOTS, PACK), at),
                pl.BlockSpec((PREFIX, 2 * HEAD_DIM), at),
            ],
            scratch_shapes=[
                pltpu.VMEM((SLOTS, KEYS + SLOTS), F32),
                pltpu.VMEM((2, SLOTS, SLOTS), F32),
                pltpu.VMEM((2, SLOTS, SLOTS), F32),
                pltpu.VMEM((KEYS + SLOTS, HEAD_DIM), BF),
                pltpu.VMEM((KEYS + SLOTS, HEAD_DIM), BF),
                pltpu.VMEM((2, PER_KV * SLOTS, HEAD_DIM), BF),
                pltpu.VMEM((2, PER_KV * SLOTS, HEAD_DIM), BF),
                pltpu.VMEM((2, HEAD_DIM, KEYS), F32),
                pltpu.VMEM((2, HEAD_DIM, KEYS), F32),
            ],
        ),
        out_shape=[shape(SLOTS, HEADS * HEAD_DIM)] * 2
        + [shape(SLOTS, KV_HEADS * HEAD_DIM)] * 2
        + [shape(SLOTS, n * PACK), shape(PREFIX, n * 2 * HEAD_DIM)],
        input_output_aliases={len(inputs) + i: i for i in range(len(bufs))},
        compiler_params=pltpu.CompilerParams(vmem_limit_bytes=50 * 2**20),
        cost_estimate=pl.CostEstimate(
            flops=n * 12 * 2048 * KEYS * HEAD_DIM, bytes_accessed=n * 4 * 2**20, transcendentals=n * 2048 * KEYS
        ),
        name="head",
    )(*inputs, *bufs)


def tie(value, *others):
    return lax.optimization_barrier((value, *others))[0]


def body(
    queries, resp_keys, resp_values, prefix_keys, prefix_values, d_out, rewards, prompt_len, resp_len, resp_assign
):
    device = lax.axis_index("resp")
    place = jnp.stack([device, device % 2]).astype(jnp.int32)
    exchange = lambda x: lax.all_to_all(x, "resp", 0, 0, tiled=True)
    swap = lambda x: lax.ppermute(x, "resp", [(i, i ^ 1) for i in range(SPREAD)])
    hop = lambda x, n: lax.ppermute(x, "prompt", [(i, (i + n) % GROUPS) for i in range(GROUPS)])

    four = resp_len + hop(resp_len, 4) + hop(resp_len, 8) + hop(resp_len, 12)
    totals = (four, hop(four, 1), hop(four, 2), hop(four, 3))
    kv = []
    for heads in PARTS:
        operand = pack_prompt(heads, prefix_keys, prefix_values)
        if kv:
            operand = tie(operand, kv[-1], *totals)
        kv.append(exchange(operand).reshape(PREFIX, -1))
    arrays = (queries, d_out, resp_keys, resp_values)
    others = tuple(swap(x) for x in arrays)

    scalars = (place, prompt_len, resp_len, resp_assign, rewards)
    bufs = []
    backs = []
    terms = []
    for heads, part in zip(PARTS, kv):
        *bufs, back, grads = head_pass(scalars, totals, arrays, others, part, heads, bufs)
        backs.append(swap(back))
        grads = grads.reshape(SPREAD, OWN, -1)
        if terms:
            grads = tie(grads, terms[-1])
        terms.append(exchange(grads))
    for heads, part in zip(PARTS, backs):
        bufs = unpack_rows(place, part, heads, bufs)
    sums = sum_terms(PARTS[0], terms[0], [])
    *bufs, dk, dv = lax.optimization_barrier((*bufs, *sums))
    return (*bufs, *sum_terms(PARTS[1], terms[1], [dk, dv]))


def solution(mesh):
    rows = P(("prompt", "resp"), None)
    return jax.shard_map(
        body,
        mesh=mesh,
        in_specs=(rows,) * 6 + (P("prompt", None), P("prompt"), P("prompt", None), P("prompt", None)),
        out_specs=(rows,) * 6,
        check_vma=False,
    )
```

```python
import functools

import jax
import jax.numpy as jnp
from jax import lax
from jax.experimental import pallas as pl
from jax.experimental.pallas import tpu as pltpu
from jax.sharding import PartitionSpec as P

HEADS = 64
KV_HEADS = 8
HEAD_DIM = 128
PER_KV = HEADS // KV_HEADS
LOCAL = KV_HEADS // 2
SLOTS = 128
OWN = 64
PREFIX = 1024
KEYS = PREFIX + SLOTS
WIDE = PER_KV * HEAD_DIM
PACK = 2 * WIDE + 2 * HEAD_DIM
TILE = 512
SCALE = HEAD_DIM**-0.5
SCALE2 = SCALE * 1.4426950408889634
SPREAD = 16
GROUPS = 16
PARTS = ((0, 1), (2, 3))

BF = jnp.bfloat16
F32 = jnp.float32
NT = (((1,), (1,)), ((), ()))
NN = (((1,), (0,)), ((), ()))
ANY = pl.BlockSpec(memory_space=pl.ANY)
SMEM = pl.BlockSpec(memory_space=pltpu.SMEM)


def dot(a, b, dims):
    return lax.dot_general(a, b, dims, preferred_element_type=F32)


def shape(*dims, dtype=BF):
    return jax.ShapeDtypeStruct(dims, dtype)


def pack_prompt_kernel(heads, k_ref, v_ref, out):
    for n, h in enumerate(heads):
        for core in range(2):
            cols = slice((core * LOCAL + h) * HEAD_DIM, (core * LOCAL + h + 1) * HEAD_DIM)
            k = k_ref[:, cols]
            v = v_ref[:, cols]
            for chip in range(SPREAD // 2):
                out[2 * chip + core, :, 2 * n * HEAD_DIM : (2 * n + 1) * HEAD_DIM] = k
                out[2 * chip + core, :, (2 * n + 1) * HEAD_DIM : (2 * n + 2) * HEAD_DIM] = v


def pack_prompt(heads, keys, values):
    return pl.pallas_call(
        functools.partial(pack_prompt_kernel, heads),
        out_shape=shape(SPREAD, OWN, len(heads) * 2 * HEAD_DIM),
        name="pack_prompt",
    )(keys, values)


def scale_of(total):
    return jnp.full((1, HEAD_DIM), 1.0 * GROUPS * SPREAD * SLOTS, F32) / jnp.sum(total[...].astype(F32))


def unpack_rows_kernel(place, total, packed, dq_in, dk_in, dv_in, _, out, dq, dk, dv):
    scale = scale_of(total)

    def scaled(dst, src):
        for j in range(dst.shape[1] // HEAD_DIM):
            cols = slice(j * HEAD_DIM, (j + 1) * HEAD_DIM)
            dst[:, cols] = (src[:, cols].astype(F32) * scale).astype(BF)

    @pl.when(pl.program_id(1) == 0)
    def _():
        out[...] = packed[:, :WIDE]
        scaled(dq, packed.at[:, WIDE : 2 * WIDE])
        scaled(dk, packed.at[:, 2 * WIDE : 2 * WIDE + HEAD_DIM])
        scaled(dv, packed.at[:, 2 * WIDE + HEAD_DIM :])

    @pl.when(pl.program_id(1) == 1)
    def _():
        scaled(dq, dq_in)
        scaled(dk, dk_in)
        scaled(dv, dv_in)


def unpack_rows(place, total, packed, heads, bufs):
    theirs = lambda h, side, place: (0, (1 - place[1]) * LOCAL + heads[0] + h)
    both = lambda h, side, place: (0, (1 - place[1] - side + 2 * side * place[1]) * LOCAL + heads[0] + h)
    wide = pl.BlockSpec((SLOTS, WIDE), both)
    narrow = pl.BlockSpec((SLOTS, HEAD_DIM), both)
    out, dq, dk, dv = bufs
    return pl.pallas_call(
        unpack_rows_kernel,
        grid_spec=pltpu.PrefetchScalarGridSpec(
            num_scalar_prefetch=1,
            grid=(len(heads), 2),
            in_specs=[
                pl.BlockSpec((1, SPREAD), lambda h, side, place: (0, 0)),
                pl.BlockSpec((SLOTS, PACK), lambda h, side, place: (0, h)),
                wide,
                narrow,
                narrow,
                ANY,
            ],
            out_specs=[pl.BlockSpec((SLOTS, WIDE), theirs), wide, narrow, narrow],
        ),
        out_shape=[shape(SLOTS, HEADS * HEAD_DIM)] * 2 + [shape(SLOTS, KV_HEADS * HEAD_DIM)] * 2,
        input_output_aliases={3: 1, 4: 2, 5: 3, 6: 0},
        name="unpack_rows",
    )(place, total, packed, dq, dk, dv, out)


def sum_terms_kernel(heads, live_total, terms, *refs):
    dk_ref, dv_ref = refs[-2:]
    scale = jnp.concatenate([scale_of(live_total)] * 2, axis=1)
    if len(refs) > 2:
        dk_ref[...] = refs[0][...]
        dv_ref[...] = refs[1][...]
    for n, h in enumerate(heads):
        cols = slice(2 * n * HEAD_DIM, (2 * n + 2) * HEAD_DIM)
        for core in range(2):
            total = terms[core, :, cols].astype(F32)
            for chip in range(1, SPREAD // 2):
                total = total + terms[2 * chip + core, :, cols].astype(F32)
            total = (total * scale).astype(BF)
            own = slice((core * LOCAL + h) * HEAD_DIM, (core * LOCAL + h + 1) * HEAD_DIM)
            dk_ref[:, own] = total[:, :HEAD_DIM]
            dv_ref[:, own] = total[:, HEAD_DIM:]


def sum_terms(heads, live_total, terms, bufs):
    return pl.pallas_call(
        functools.partial(sum_terms_kernel, heads),
        in_specs=[pl.BlockSpec(memory_space=pltpu.VMEM)] * (2 + len(bufs)),
        out_shape=[shape(OWN, KV_HEADS * HEAD_DIM)] * 2,
        name="sum_terms",
    )(live_total, terms, *bufs)


def head_kernel(n_alias, place, prompt_len, resp_len, resp_assign, rewards, *refs):
    q_ref, do_ref, kr_ref, vr_ref, q2_ref, do2_ref, kr2_ref, vr2_ref, kv_ref = refs[:9]
    out_ref, dq_ref, dkr_ref, dvr_ref, back, grads = refs[9 + n_alias : 15 + n_alias]
    bias, weight, live, ks, vs, qs, cs, dka, dva = refs[15 + n_alias :]

    @pl.when(pl.program_id(0) == 0)
    def _():
        key = lax.broadcasted_iota(jnp.int32, (SLOTS, PREFIX), 1)
        row = lax.broadcasted_iota(jnp.int32, (SLOTS, SLOTS), 0)
        col = lax.broadcasted_iota(jnp.int32, (SLOTS, SLOTS), 1)
        resp_bias = jnp.where(col <= row, 0.0, -jnp.inf)
        bias[:, :SLOTS] = resp_bias
        bias[:, SLOTS:KEYS] = jnp.where(key < prompt_len[0], 0.0, -jnp.inf)
        bias[:, KEYS:] = resp_bias
        mean = rewards[0, 0]
        for i in range(1, SPREAD):
            mean = mean + rewards[0, i]
        mean = mean * (1.0 / SPREAD)
        for b in range(2):
            device = place[0] if b == 0 else place[0] + 1 - 2 * place[1]
            length = 0
            advantage = 0.0
            for i in range(SPREAD):
                here = resp_assign[0, i] == device
                length = length + jnp.where(here, resp_len[0, i], 0)
                advantage = advantage + jnp.where(here, rewards[0, i] - mean, 0.0)
            alive = jnp.where(row < length, 1.0, 0.0)
            live[b] = alive
            weight[b] = -advantage * alive

    ks[:SLOTS, :] = kr_ref[...]
    ks[SLOTS:KEYS, :] = kv_ref[:, :HEAD_DIM]
    ks[KEYS:, :] = kr2_ref[...]
    vs[:SLOTS, :] = vr_ref[...]
    vs[SLOTS:KEYS, :] = kv_ref[:, HEAD_DIM:]
    vs[KEYS:, :] = vr2_ref[...]
    for b, (q, do) in enumerate(((q_ref, do_ref), (q2_ref, do2_ref))):
        w = weight[b]
        for j in range(PER_KV):
            cols = slice(j * HEAD_DIM, (j + 1) * HEAD_DIM)
            rows = slice(j * SLOTS, (j + 1) * SLOTS)
            qs[b, rows, :] = q[:, cols]
            cs[b, rows, :] = (do[:, cols].astype(F32) * w).astype(BF)

    per = TILE // SLOTS
    tiles = PER_KV * SLOTS // TILE
    units = [(b, t) for b in range(2) for t in range(tiles)]
    spans = (slice(0, KEYS), slice(SLOTS, SLOTS + KEYS))

    def store(b, t, value, own, start):
        for i in range(per):
            j = t * per + i
            piece = value[i * SLOTS : (i + 1) * SLOTS]
            if b == 0:
                own[:, j * HEAD_DIM : (j + 1) * HEAD_DIM] = piece
            else:
                back[:, start + j * HEAD_DIM : start + (j + 1) * HEAD_DIM] = piece

    def softmax_part(b, t):
        rows = slice(t * TILE, (t + 1) * TILE)
        s = dot(qs[b, rows, :], ks[spans[b], :], NT)
        s = s + jnp.concatenate([bias[:, spans[b]]] * per, axis=0)
        m = jnp.max(s, axis=1, keepdims=True)
        p = jnp.exp2(s * SCALE2 - m * SCALE2)
        return p, 1.0 / jnp.sum(p, axis=1, keepdims=True)

    def score_part(b, t, p, inv):
        rows = slice(t * TILE, (t + 1) * TILE)
        c = cs[b, rows, :]
        att = p * inv
        ab = att.astype(BF)
        alive = jnp.concatenate([live[b]] * per, axis=0)
        ob = (dot(ab, vs[spans[b], :], NN) * alive).astype(BF)
        row_dot = jnp.sum(c.astype(F32) * ob.astype(F32), axis=1, keepdims=True)
        dp = dot(c, vs[spans[b], :], NT)
        ds = (att * (dp - row_dot)).astype(BF)
        store(b, t, ob, out_ref, 0)
        return ab, ds

    def grad_part(b, t, ab, ds):
        rows = slice(t * TILE, (t + 1) * TILE)
        store(b, t, (dot(ds, ks[spans[b], :], NN) * SCALE).astype(BF), dq_ref, WIDE)
        dv = dot(cs[b, rows, :].T, ab, NN)
        dk = dot(qs[b, rows, :].T, ds, NN)
        if t > 0:
            dv = dv + dva[b]
            dk = dk + dka[b]
        dva[b] = dv
        dka[b] = dk

    now = softmax_part(*units[0])
    last = None
    for u, unit in enumerate(units):
        later = softmax_part(*units[u + 1]) if u + 1 < len(units) else None
        if last is not None:
            grad_part(*units[u - 1], *last)
        last = score_part(*unit, *now)
        now = later
    grad_part(*units[-1], *last)

    dkr_ref[...] = (dka[0, :, :SLOTS] * SCALE).T.astype(BF)
    dvr_ref[...] = dva[0, :, :SLOTS].T.astype(BF)
    back[:, 2 * WIDE : 2 * WIDE + HEAD_DIM] = (dka[1, :, PREFIX:] * SCALE).T.astype(BF)
    back[:, 2 * WIDE + HEAD_DIM :] = dva[1, :, PREFIX:].T.astype(BF)
    grads[:, :HEAD_DIM] = ((dka[0, :, SLOTS:] + dka[1, :, :PREFIX]) * SCALE).T.astype(BF)
    grads[:, HEAD_DIM:] = (dva[0, :, SLOTS:] + dva[1, :, :PREFIX]).T.astype(BF)


def head_pass(scalars, arrays, others, kv, heads, bufs):
    mine = lambda g, place: (0, place[1] * LOCAL + heads[0] + g)
    at = lambda g, place: (0, g)
    wide = pl.BlockSpec((SLOTS, WIDE), mine)
    narrow = pl.BlockSpec((SLOTS, HEAD_DIM), mine)
    inputs = (*scalars, *arrays, *others, kv)
    n = len(heads)
    return pl.pallas_call(
        functools.partial(head_kernel, len(bufs)),
        grid_spec=pltpu.PrefetchScalarGridSpec(
            num_scalar_prefetch=1,
            grid=(n,),
            in_specs=[SMEM] * 4
            + [wide, wide, narrow, narrow] * 2
            + [pl.BlockSpec((PREFIX, 2 * HEAD_DIM), at)]
            + [ANY] * len(bufs),
            out_specs=[
                wide,
                wide,
                narrow,
                narrow,
                pl.BlockSpec((SLOTS, PACK), at),
                pl.BlockSpec((PREFIX, 2 * HEAD_DIM), at),
            ],
            scratch_shapes=[
                pltpu.VMEM((SLOTS, KEYS + SLOTS), F32),
                pltpu.VMEM((2, SLOTS, SLOTS), F32),
                pltpu.VMEM((2, SLOTS, SLOTS), F32),
                pltpu.VMEM((KEYS + SLOTS, HEAD_DIM), BF),
                pltpu.VMEM((KEYS + SLOTS, HEAD_DIM), BF),
                pltpu.VMEM((2, PER_KV * SLOTS, HEAD_DIM), BF),
                pltpu.VMEM((2, PER_KV * SLOTS, HEAD_DIM), BF),
                pltpu.VMEM((2, HEAD_DIM, KEYS), F32),
                pltpu.VMEM((2, HEAD_DIM, KEYS), F32),
            ],
        ),
        out_shape=[shape(SLOTS, HEADS * HEAD_DIM)] * 2
        + [shape(SLOTS, KV_HEADS * HEAD_DIM)] * 2
        + [shape(SLOTS, n * PACK), shape(PREFIX, n * 2 * HEAD_DIM)],
        input_output_aliases={len(inputs) + i: i for i in range(len(bufs))},
        compiler_params=pltpu.CompilerParams(vmem_limit_bytes=50 * 2**20),
        cost_estimate=pl.CostEstimate(
            flops=n * 12 * 2048 * KEYS * HEAD_DIM, bytes_accessed=n * 4 * 2**20, transcendentals=n * 2048 * KEYS
        ),
        name="head",
    )(*inputs, *bufs)


def tie(value, *others):
    return lax.optimization_barrier((value, *others))[0]


def body(
    queries, resp_keys, resp_values, prefix_keys, prefix_values, d_out, rewards, prompt_len, resp_len, resp_assign
):
    device = lax.axis_index("resp")
    place = jnp.stack([device, device % 2]).astype(jnp.int32)
    exchange = lambda x: lax.all_to_all(x, "resp", 0, 0, tiled=True)
    swap = lambda x: lax.ppermute(x, "resp", [(i, i ^ 1) for i in range(SPREAD)])
    hop = lambda x, n: lax.ppermute(x, "prompt", [(i, (i + n) % GROUPS) for i in range(GROUPS)])

    arrays = (queries, d_out, resp_keys, resp_values)
    others = tuple(swap(x) for x in arrays)
    total = resp_len + hop(resp_len, 8)
    total = total + hop(total, 4)
    kv = [exchange(pack_prompt(PARTS[0], prefix_keys, prefix_values))]
    later = tie(pack_prompt(PARTS[1], prefix_keys, prefix_values), kv[0], total, *others)
    kv.append(exchange(later))

    scalars = (place, prompt_len, resp_len, resp_assign, rewards)
    bufs = []
    backs = []
    terms = []
    for heads, part, far in zip(PARTS, kv, (2, 1)):
        step = hop(total, far)
        *bufs, back, grads = head_pass(scalars, arrays, others, part.reshape(PREFIX, -1), heads, bufs)
        total = total + tie(step, grads)
        backs.append(swap(back))
        grads = grads.reshape(SPREAD, OWN, -1)
        if terms:
            grads = tie(grads, terms[-1])
        terms.append(exchange(grads))
    for heads, part in zip(PARTS, backs):
        bufs = unpack_rows(place, total, part, heads, bufs)
    sums = sum_terms(PARTS[0], total, terms[0], [])
    *bufs, dk, dv = lax.optimization_barrier((*bufs, *sums))
    return (*bufs, *sum_terms(PARTS[1], total, terms[1], [dk, dv]))


def solution(mesh):
    rows = P(("prompt", "resp"), None)
    return jax.shard_map(
        body,
        mesh=mesh,
        in_specs=(rows,) * 6 + (P("prompt", None), P("prompt"), P("prompt", None), P("prompt", None)),
        out_specs=(rows,) * 6,
        check_vma=False,
    )
```

```python
import functools

import jax
import jax.numpy as jnp
from jax import lax
from jax.experimental import pallas as pl
from jax.experimental.pallas import tpu as pltpu
from jax.sharding import PartitionSpec as P

HEADS = 64
KV_HEADS = 8
HEAD_DIM = 128
PER_KV = HEADS // KV_HEADS
LOCAL = KV_HEADS // 2
SLOTS = 128
OWN = 64
PREFIX = 1024
KEYS = PREFIX + SLOTS
WIDE = PER_KV * HEAD_DIM
PACK = 2 * WIDE + 2 * HEAD_DIM
TILE = 512
SCALE = HEAD_DIM**-0.5
SCALE2 = SCALE * 1.4426950408889634
SPREAD = 16
GROUPS = 16
PARTS = ((0, 1), (2, 3))
RIDER = 16

BF = jnp.bfloat16
F32 = jnp.float32
NT = (((1,), (1,)), ((), ()))
NN = (((1,), (0,)), ((), ()))
ANY = pl.BlockSpec(memory_space=pl.ANY)
SMEM = pl.BlockSpec(memory_space=pltpu.SMEM)


def dot(a, b, dims):
    return lax.dot_general(a, b, dims, preferred_element_type=F32)


def shape(*dims, dtype=BF):
    return jax.ShapeDtypeStruct(dims, dtype)


def pack_prompt_kernel(heads, k_ref, v_ref, *refs):
    out = refs[-1]
    for n, h in enumerate(heads):
        for core in range(2):
            cols = slice((core * LOCAL + h) * HEAD_DIM, (core * LOCAL + h + 1) * HEAD_DIM)
            k = k_ref[:, cols]
            v = v_ref[:, cols]
            for chip in range(SPREAD // 2):
                out[2 * chip + core, :OWN, 2 * n * HEAD_DIM : (2 * n + 1) * HEAD_DIM] = k
                out[2 * chip + core, :OWN, (2 * n + 1) * HEAD_DIM : (2 * n + 2) * HEAD_DIM] = v
    if len(refs) > 1:
        lens = refs[0][...]
        for device in range(SPREAD):
            out[device, OWN:, :HEAD_DIM] = lens
            out[device, OWN:, HEAD_DIM:] = jnp.zeros((RIDER, (2 * len(heads) - 1) * HEAD_DIM), BF)


def pack_prompt(heads, keys, values, *lens):
    return pl.pallas_call(
        functools.partial(pack_prompt_kernel, heads),
        out_shape=shape(SPREAD, OWN + RIDER * len(lens), len(heads) * 2 * HEAD_DIM),
        name="pack_prompt",
    )(keys, values, *lens)


def scale_of(total):
    return jnp.full((1, HEAD_DIM), 1.0 * GROUPS * SPREAD * SLOTS, F32) / total[:1, :]


def unpack_rows_kernel(place, packed, *refs):
    out, dq, dk, dv = refs[-4:]
    out[...] = packed[:, :WIDE]
    dq[...] = packed[:, WIDE : 2 * WIDE]
    dk[...] = packed[:, 2 * WIDE : 2 * WIDE + HEAD_DIM]
    dv[...] = packed[:, 2 * WIDE + HEAD_DIM :]


def unpack_rows(place, packed, heads, bufs):
    theirs = lambda h, place: (0, (1 - place[1]) * LOCAL + heads[0] + h)
    wide = pl.BlockSpec((SLOTS, WIDE), theirs)
    narrow = pl.BlockSpec((SLOTS, HEAD_DIM), theirs)
    return pl.pallas_call(
        unpack_rows_kernel,
        grid_spec=pltpu.PrefetchScalarGridSpec(
            num_scalar_prefetch=1,
            grid=(len(heads),),
            in_specs=[pl.BlockSpec((SLOTS, PACK), lambda h, place: (0, h))] + [ANY] * 4,
            out_specs=[wide, wide, narrow, narrow],
        ),
        out_shape=[shape(SLOTS, HEADS * HEAD_DIM)] * 2 + [shape(SLOTS, KV_HEADS * HEAD_DIM)] * 2,
        input_output_aliases={2 + i: i for i in range(4)},
        name="unpack_rows",
    )(place, packed, *bufs)


def scale_rows_kernel(place, total, packed, dq_in, dk_in, dv_in, _, out, dq, dk, dv):
    scale = scale_of(total)

    def scaled(dst, src):
        for j in range(dst.shape[1] // HEAD_DIM):
            cols = slice(j * HEAD_DIM, (j + 1) * HEAD_DIM)
            dst[:, cols] = (src[:, cols].astype(F32) * scale).astype(BF)

    @pl.when(pl.program_id(1) == 0)
    def _():
        out[...] = packed[:, :WIDE]
        scaled(dq, packed.at[:, WIDE : 2 * WIDE])
        scaled(dk, packed.at[:, 2 * WIDE : 2 * WIDE + HEAD_DIM])
        scaled(dv, packed.at[:, 2 * WIDE + HEAD_DIM :])

    @pl.when(pl.program_id(1) == 1)
    def _():
        scaled(dq, dq_in)
        scaled(dk, dk_in)
        scaled(dv, dv_in)


def scale_rows(place, total, packed, heads, bufs):
    theirs = lambda h, side, place: (0, (1 - place[1]) * LOCAL + heads[0] + h)
    both = lambda h, side, place: (0, (1 - place[1] - side + 2 * side * place[1]) * LOCAL + heads[0] + h)
    wide = pl.BlockSpec((SLOTS, WIDE), both)
    narrow = pl.BlockSpec((SLOTS, HEAD_DIM), both)
    out, dq, dk, dv = bufs
    return pl.pallas_call(
        scale_rows_kernel,
        grid_spec=pltpu.PrefetchScalarGridSpec(
            num_scalar_prefetch=1,
            grid=(len(heads), 2),
            in_specs=[
                pl.BlockSpec((8, HEAD_DIM), lambda h, side, place: (0, 0)),
                pl.BlockSpec((SLOTS, PACK), lambda h, side, place: (0, h)),
                wide,
                narrow,
                narrow,
                ANY,
            ],
            out_specs=[pl.BlockSpec((SLOTS, WIDE), theirs), wide, narrow, narrow],
        ),
        out_shape=[shape(SLOTS, HEADS * HEAD_DIM)] * 2 + [shape(SLOTS, KV_HEADS * HEAD_DIM)] * 2,
        input_output_aliases={3: 1, 4: 2, 5: 3, 6: 0},
        name="scale_rows",
    )(place, total, packed, dq, dk, dv, out)


def sum_terms_kernel(heads, scaled, *refs):
    dk_ref, dv_ref = refs[-2:]
    if scaled:
        live_total, terms = refs[:2]
        scale = jnp.concatenate([scale_of(live_total)] * 2, axis=1)
    else:
        terms = refs[0]
        dk_ref[...] = refs[1][...]
        dv_ref[...] = refs[2][...]
    for n, h in enumerate(heads):
        cols = slice(2 * n * HEAD_DIM, (2 * n + 2) * HEAD_DIM)
        for core in range(2):
            total = terms[core, :, cols].astype(F32)
            for chip in range(1, SPREAD // 2):
                total = total + terms[2 * chip + core, :, cols].astype(F32)
            if scaled:
                total = total * scale
            total = total.astype(BF)
            own = slice((core * LOCAL + h) * HEAD_DIM, (core * LOCAL + h + 1) * HEAD_DIM)
            dk_ref[:, own] = total[:, :HEAD_DIM]
            dv_ref[:, own] = total[:, HEAD_DIM:]


def sum_terms(heads, scaled, *inputs):
    return pl.pallas_call(
        functools.partial(sum_terms_kernel, heads, scaled),
        out_shape=[shape(OWN, KV_HEADS * HEAD_DIM)] * 2,
        name="sum_terms",
    )(*inputs)


def head_kernel(n_alias, rider, place, prompt_len, resp_len, resp_assign, rewards, *refs):
    q_ref, do_ref, kr_ref, vr_ref, q2_ref, do2_ref, kr2_ref, vr2_ref, kv_ref = refs[:9]
    out_ref, dq_ref, dkr_ref, dvr_ref, back, grads, *live_total = refs[9 + n_alias : 15 + n_alias + (rider > 0)]
    bias, weight, live, ks, vs, qs, cs, dka, dva = refs[15 + n_alias + (rider > 0) :]
    stride = OWN + rider

    @pl.when(pl.program_id(0) == 0)
    def _():
        key = lax.broadcasted_iota(jnp.int32, (SLOTS, PREFIX), 1)
        row = lax.broadcasted_iota(jnp.int32, (SLOTS, SLOTS), 0)
        col = lax.broadcasted_iota(jnp.int32, (SLOTS, SLOTS), 1)
        resp_bias = jnp.where(col <= row, 0.0, -jnp.inf)
        bias[:, :SLOTS] = resp_bias
        bias[:, SLOTS:KEYS] = jnp.where(key < prompt_len[0], 0.0, -jnp.inf)
        bias[:, KEYS:] = resp_bias
        mean = rewards[0, 0]
        for i in range(1, SPREAD):
            mean = mean + rewards[0, i]
        mean = mean * (1.0 / SPREAD)
        if rider:
            total = jnp.zeros((rider, HEAD_DIM), F32)
            for d in range(SPREAD):
                total = total + kv_ref[d * stride + OWN : (d + 1) * stride, :HEAD_DIM].astype(F32)
            live_total[0][...] = jnp.full((8, HEAD_DIM), jnp.sum(total), F32)
        for b in range(2):
            device = place[0] if b == 0 else place[0] + 1 - 2 * place[1]
            length = 0
            advantage = 0.0
            for i in range(SPREAD):
                here = resp_assign[0, i] == device
                length = length + jnp.where(here, resp_len[0, i], 0)
                advantage = advantage + jnp.where(here, rewards[0, i] - mean, 0.0)
            alive = jnp.where(row < length, 1.0, 0.0)
            live[b] = alive
            weight[b] = -advantage * alive
            if rider:
                weight[b] = -scale_of(live_total[0]) * (advantage * alive)

    ks[:SLOTS, :] = kr_ref[...]
    ks[KEYS:, :] = kr2_ref[...]
    vs[:SLOTS, :] = vr_ref[...]
    vs[KEYS:, :] = vr2_ref[...]
    for d in range(SPREAD):
        rows = slice(SLOTS + d * OWN, SLOTS + (d + 1) * OWN)
        ks[rows, :] = kv_ref[d * stride : d * stride + OWN, :HEAD_DIM]
        vs[rows, :] = kv_ref[d * stride : d * stride + OWN, HEAD_DIM:]
    for b, (q, do) in enumerate(((q_ref, do_ref), (q2_ref, do2_ref))):
        w = weight[b]
        for j in range(PER_KV):
            cols = slice(j * HEAD_DIM, (j + 1) * HEAD_DIM)
            rows = slice(j * SLOTS, (j + 1) * SLOTS)
            qs[b, rows, :] = q[:, cols]
            cs[b, rows, :] = (do[:, cols].astype(F32) * w).astype(BF)

    per = TILE // SLOTS
    tiles = PER_KV * SLOTS // TILE
    units = [(b, t) for b in range(2) for t in range(tiles)]
    spans = (slice(0, KEYS), slice(SLOTS, SLOTS + KEYS))

    def store(b, t, value, own, start):
        for i in range(per):
            j = t * per + i
            piece = value[i * SLOTS : (i + 1) * SLOTS]
            if b == 0:
                own[:, j * HEAD_DIM : (j + 1) * HEAD_DIM] = piece
            else:
                back[:, start + j * HEAD_DIM : start + (j + 1) * HEAD_DIM] = piece

    def softmax_part(b, t):
        rows = slice(t * TILE, (t + 1) * TILE)
        s = dot(qs[b, rows, :], ks[spans[b], :], NT)
        s = s + jnp.concatenate([bias[:, spans[b]]] * per, axis=0)
        m = jnp.max(s, axis=1, keepdims=True)
        p = jnp.exp2(s * SCALE2 - m * SCALE2)
        return p, 1.0 / jnp.sum(p, axis=1, keepdims=True)

    def score_part(b, t, p, inv):
        rows = slice(t * TILE, (t + 1) * TILE)
        c = cs[b, rows, :]
        att = p * inv
        ab = att.astype(BF)
        alive = jnp.concatenate([live[b]] * per, axis=0)
        ob = (dot(ab, vs[spans[b], :], NN) * alive).astype(BF)
        row_dot = jnp.sum(c.astype(F32) * ob.astype(F32), axis=1, keepdims=True)
        dp = dot(c, vs[spans[b], :], NT)
        ds = (att * (dp - row_dot)).astype(BF)
        store(b, t, ob, out_ref, 0)
        return ab, ds

    def grad_part(b, t, ab, ds):
        rows = slice(t * TILE, (t + 1) * TILE)
        store(b, t, (dot(ds, ks[spans[b], :], NN) * SCALE).astype(BF), dq_ref, WIDE)
        dv = dot(cs[b, rows, :].T, ab, NN)
        dk = dot(qs[b, rows, :].T, ds, NN)
        if t > 0:
            dv = dv + dva[b]
            dk = dk + dka[b]
        dva[b] = dv
        dka[b] = dk

    now = softmax_part(*units[0])
    last = None
    for u, unit in enumerate(units):
        later = softmax_part(*units[u + 1]) if u + 1 < len(units) else None
        if last is not None:
            grad_part(*units[u - 1], *last)
        last = score_part(*unit, *now)
        now = later
    grad_part(*units[-1], *last)

    dkr_ref[...] = (dka[0, :, :SLOTS] * SCALE).T.astype(BF)
    dvr_ref[...] = dva[0, :, :SLOTS].T.astype(BF)
    back[:, 2 * WIDE : 2 * WIDE + HEAD_DIM] = (dka[1, :, PREFIX:] * SCALE).T.astype(BF)
    back[:, 2 * WIDE + HEAD_DIM :] = dva[1, :, PREFIX:].T.astype(BF)
    grads[:, :HEAD_DIM] = ((dka[0, :, SLOTS:] + dka[1, :, :PREFIX]) * SCALE).T.astype(BF)
    grads[:, HEAD_DIM:] = (dva[0, :, SLOTS:] + dva[1, :, :PREFIX]).T.astype(BF)


def head_pass(scalars, arrays, others, kv, heads, bufs):
    mine = lambda g, place: (0, place[1] * LOCAL + heads[0] + g)
    at = lambda g, place: (0, g)
    wide = pl.BlockSpec((SLOTS, WIDE), mine)
    narrow = pl.BlockSpec((SLOTS, HEAD_DIM), mine)
    inputs = (*scalars, *arrays, *others, kv)
    n = len(heads)
    rider = kv.shape[0] // SPREAD - OWN
    extra = rider > 0
    return pl.pallas_call(
        functools.partial(head_kernel, len(bufs), rider),
        grid_spec=pltpu.PrefetchScalarGridSpec(
            num_scalar_prefetch=1,
            grid=(n,),
            in_specs=[SMEM] * 4
            + [wide, wide, narrow, narrow] * 2
            + [pl.BlockSpec((kv.shape[0], 2 * HEAD_DIM), at)]
            + [ANY] * len(bufs),
            out_specs=[
                wide,
                wide,
                narrow,
                narrow,
                pl.BlockSpec((SLOTS, PACK), at),
                pl.BlockSpec((PREFIX, 2 * HEAD_DIM), at),
            ]
            + [pl.BlockSpec((8, HEAD_DIM), lambda g, place: (0, 0))] * extra,
            scratch_shapes=[
                pltpu.VMEM((SLOTS, KEYS + SLOTS), F32),
                pltpu.VMEM((2, SLOTS, SLOTS), F32),
                pltpu.VMEM((2, SLOTS, SLOTS), F32),
                pltpu.VMEM((KEYS + SLOTS, HEAD_DIM), BF),
                pltpu.VMEM((KEYS + SLOTS, HEAD_DIM), BF),
                pltpu.VMEM((2, PER_KV * SLOTS, HEAD_DIM), BF),
                pltpu.VMEM((2, PER_KV * SLOTS, HEAD_DIM), BF),
                pltpu.VMEM((2, HEAD_DIM, KEYS), F32),
                pltpu.VMEM((2, HEAD_DIM, KEYS), F32),
            ],
        ),
        out_shape=[shape(SLOTS, HEADS * HEAD_DIM)] * 2
        + [shape(SLOTS, KV_HEADS * HEAD_DIM)] * 2
        + [shape(SLOTS, n * PACK), shape(PREFIX, n * 2 * HEAD_DIM)]
        + [shape(8, HEAD_DIM, dtype=F32)] * extra,
        input_output_aliases={len(inputs) + i: i for i in range(len(bufs))},
        compiler_params=pltpu.CompilerParams(vmem_limit_bytes=50 * 2**20),
        cost_estimate=pl.CostEstimate(
            flops=n * 12 * 2048 * KEYS * HEAD_DIM, bytes_accessed=n * 4 * 2**20, transcendentals=n * 2048 * KEYS
        ),
        name="head",
    )(*inputs, *bufs)


def tie(value, *others):
    return lax.optimization_barrier((value, *others))[0]


def body(
    queries, resp_keys, resp_values, prefix_keys, prefix_values, d_out, rewards, prompt_len, resp_len, resp_assign
):
    device = lax.axis_index("resp")
    place = jnp.stack([device, device % 2]).astype(jnp.int32)
    exchange = lambda x: lax.all_to_all(x, "resp", 0, 0, tiled=True)
    swap = lambda x: lax.ppermute(x, "resp", [(i, i ^ 1) for i in range(SPREAD)])
    spread = [(p * SPREAD + r, (p + r) % GROUPS * SPREAD + r) for p in range(GROUPS) for r in range(SPREAD)]
    lens = lax.ppermute(resp_len, ("prompt", "resp"), spread)

    arrays = (queries, d_out, resp_keys, resp_values)
    others = tuple(swap(x) for x in arrays)
    kv = exchange(pack_prompt(PARTS[0], prefix_keys, prefix_values))
    lens = jnp.pad(lens.astype(BF), ((0, RIDER - 1), (0, HEAD_DIM - SPREAD)))
    later = tie(pack_prompt(PARTS[1], prefix_keys, prefix_values, lens), kv, *others)
    kv_later = exchange(later)

    scalars = (place, prompt_len, resp_len, resp_assign, rewards)
    *bufs, back, grads = head_pass(scalars, arrays, others, kv.reshape(PREFIX, -1), PARTS[0], [])
    terms = exchange(grads.reshape(SPREAD, OWN, -1))
    returned = swap(back)
    kv_later = kv_later.reshape(SPREAD * (OWN + RIDER), -1)
    *bufs, back, grads, total = head_pass(scalars, arrays, others, kv_later, PARTS[1], bufs)
    last_terms = exchange(tie(grads.reshape(SPREAD, OWN, -1), terms))
    last_returned = swap(back)

    sums = sum_terms(PARTS[0], True, total, terms)
    bufs = scale_rows(place, total, returned, PARTS[0], bufs)
    bufs = unpack_rows(place, last_returned, PARTS[1], bufs)
    *bufs, dk, dv = lax.optimization_barrier((*bufs, *sums))
    return (*bufs, *sum_terms(PARTS[1], False, last_terms, dk, dv))


def solution(mesh):
    rows = P(("prompt", "resp"), None)
    return jax.shard_map(
        body,
        mesh=mesh,
        in_specs=(rows,) * 6 + (P("prompt", None), P("prompt"), P("prompt", None), P("prompt", None)),
        out_specs=(rows,) * 6,
        check_vma=False,
    )
```

```python
import functools

import jax
import jax.numpy as jnp
from jax import lax
from jax.experimental import pallas as pl
from jax.experimental.pallas import tpu as pltpu
from jax.sharding import PartitionSpec as P

HEADS = 64
KV_HEADS = 8
HEAD_DIM = 128
PER_KV = HEADS // KV_HEADS
LOCAL = KV_HEADS // 2
SLOTS = 128
OWN = 64
PREFIX = 1024
KEYS = PREFIX + SLOTS
WIDE = PER_KV * HEAD_DIM
PACK = 2 * WIDE + 2 * HEAD_DIM
TILE = 512
SCALE = HEAD_DIM**-0.5
SCALE2 = SCALE * 1.4426950408889634
SPREAD = 16
GROUPS = 16
PARTS = ((0, 1), (2, 3))
RIDER = 16

BF = jnp.bfloat16
F32 = jnp.float32
NT = (((1,), (1,)), ((), ()))
NN = (((1,), (0,)), ((), ()))
ANY = pl.BlockSpec(memory_space=pl.ANY)
SMEM = pl.BlockSpec(memory_space=pltpu.SMEM)


def dot(a, b, dims):
    return lax.dot_general(a, b, dims, preferred_element_type=F32)


def shape(*dims, dtype=BF):
    return jax.ShapeDtypeStruct(dims, dtype)


def pack_prompt_kernel(heads, k_ref, v_ref, *refs):
    out = refs[-1]
    for n, h in enumerate(heads):
        for core in range(2):
            cols = slice((core * LOCAL + h) * HEAD_DIM, (core * LOCAL + h + 1) * HEAD_DIM)
            k = k_ref[:, cols]
            v = v_ref[:, cols]
            for chip in range(SPREAD // 2):
                out[2 * chip + core, :OWN, 2 * n * HEAD_DIM : (2 * n + 1) * HEAD_DIM] = k
                out[2 * chip + core, :OWN, (2 * n + 1) * HEAD_DIM : (2 * n + 2) * HEAD_DIM] = v
    if len(refs) > 1:
        lens = refs[0][...]
        for device in range(SPREAD):
            out[device, OWN:, :HEAD_DIM] = lens
            out[device, OWN:, HEAD_DIM:] = jnp.zeros((RIDER, (2 * len(heads) - 1) * HEAD_DIM), BF)


def pack_prompt(heads, keys, values, *lens):
    return pl.pallas_call(
        functools.partial(pack_prompt_kernel, heads),
        out_shape=shape(SPREAD, OWN + RIDER * len(lens), len(heads) * 2 * HEAD_DIM),
        compiler_params=pltpu.CompilerParams(vmem_limit_bytes=16 * 2**20),
        name="pack_prompt",
    )(keys, values, *lens)


def scale_of(total):
    return jnp.full((1, HEAD_DIM), 1.0 * GROUPS * SPREAD * SLOTS, F32) / total[:1, :]


def unpack_rows_kernel(place, packed, *refs):
    out, dq, dk, dv = refs[-4:]
    out[...] = packed[:, :WIDE]
    dq[...] = packed[:, WIDE : 2 * WIDE]
    dk[...] = packed[:, 2 * WIDE : 2 * WIDE + HEAD_DIM]
    dv[...] = packed[:, 2 * WIDE + HEAD_DIM :]


def unpack_rows(place, packed, heads, bufs):
    theirs = lambda h, place: (0, (1 - place[1]) * LOCAL + heads[0] + h)
    wide = pl.BlockSpec((SLOTS, WIDE), theirs)
    narrow = pl.BlockSpec((SLOTS, HEAD_DIM), theirs)
    return pl.pallas_call(
        unpack_rows_kernel,
        grid_spec=pltpu.PrefetchScalarGridSpec(
            num_scalar_prefetch=1,
            grid=(len(heads),),
            in_specs=[pl.BlockSpec((SLOTS, PACK), lambda h, place: (0, h))] + [ANY] * 4,
            out_specs=[wide, wide, narrow, narrow],
        ),
        out_shape=[shape(SLOTS, HEADS * HEAD_DIM)] * 2 + [shape(SLOTS, KV_HEADS * HEAD_DIM)] * 2,
        input_output_aliases={2 + i: i for i in range(4)},
        name="unpack_rows",
    )(place, packed, *bufs)


def scale_rows_kernel(place, total, packed, dq_in, dk_in, dv_in, _, out, dq, dk, dv):
    scale = scale_of(total)

    def scaled(dst, src):
        for j in range(dst.shape[1] // HEAD_DIM):
            cols = slice(j * HEAD_DIM, (j + 1) * HEAD_DIM)
            dst[:, cols] = (src[:, cols].astype(F32) * scale).astype(BF)

    @pl.when(pl.program_id(1) == 0)
    def _():
        out[...] = packed[:, :WIDE]
        scaled(dq, packed.at[:, WIDE : 2 * WIDE])
        scaled(dk, packed.at[:, 2 * WIDE : 2 * WIDE + HEAD_DIM])
        scaled(dv, packed.at[:, 2 * WIDE + HEAD_DIM :])

    @pl.when(pl.program_id(1) == 1)
    def _():
        scaled(dq, dq_in)
        scaled(dk, dk_in)
        scaled(dv, dv_in)


def scale_rows(place, total, packed, heads, bufs):
    theirs = lambda h, side, place: (0, (1 - place[1]) * LOCAL + heads[0] + h)
    both = lambda h, side, place: (0, (1 - place[1] - side + 2 * side * place[1]) * LOCAL + heads[0] + h)
    wide = pl.BlockSpec((SLOTS, WIDE), both)
    narrow = pl.BlockSpec((SLOTS, HEAD_DIM), both)
    out, dq, dk, dv = bufs
    return pl.pallas_call(
        scale_rows_kernel,
        grid_spec=pltpu.PrefetchScalarGridSpec(
            num_scalar_prefetch=1,
            grid=(len(heads), 2),
            in_specs=[
                pl.BlockSpec((8, HEAD_DIM), lambda h, side, place: (0, 0)),
                pl.BlockSpec((SLOTS, PACK), lambda h, side, place: (0, h)),
                wide,
                narrow,
                narrow,
                ANY,
            ],
            out_specs=[pl.BlockSpec((SLOTS, WIDE), theirs), wide, narrow, narrow],
        ),
        out_shape=[shape(SLOTS, HEADS * HEAD_DIM)] * 2 + [shape(SLOTS, KV_HEADS * HEAD_DIM)] * 2,
        input_output_aliases={3: 1, 4: 2, 5: 3, 6: 0},
        name="scale_rows",
    )(place, total, packed, dq, dk, dv, out)


def sum_terms_kernel(heads, scaled, *refs):
    dk_ref, dv_ref = refs[-2:]
    if scaled:
        live_total, terms = refs[:2]
        scale = jnp.concatenate([scale_of(live_total)] * 2, axis=1)
    else:
        terms = refs[0]
        dk_ref[...] = refs[1][...]
        dv_ref[...] = refs[2][...]
    for n, h in enumerate(heads):
        cols = slice(2 * n * HEAD_DIM, (2 * n + 2) * HEAD_DIM)
        for core in range(2):
            total = terms[core, :, cols].astype(F32)
            for chip in range(1, SPREAD // 2):
                total = total + terms[2 * chip + core, :, cols].astype(F32)
            if scaled:
                total = total * scale
            total = total.astype(BF)
            own = slice((core * LOCAL + h) * HEAD_DIM, (core * LOCAL + h + 1) * HEAD_DIM)
            dk_ref[:, own] = total[:, :HEAD_DIM]
            dv_ref[:, own] = total[:, HEAD_DIM:]


def sum_terms(heads, scaled, *inputs):
    return pl.pallas_call(
        functools.partial(sum_terms_kernel, heads, scaled),
        out_shape=[shape(OWN, KV_HEADS * HEAD_DIM)] * 2,
        compiler_params=pltpu.CompilerParams(vmem_limit_bytes=16 * 2**20),
        name="sum_terms",
    )(*inputs)


def head_kernel(n_alias, rider, place, prompt_len, resp_len, resp_assign, rewards, *refs):
    q_ref, do_ref, kr_ref, vr_ref, q2_ref, do2_ref, kr2_ref, vr2_ref, kv_ref = refs[:9]
    out_ref, dq_ref, dkr_ref, dvr_ref, back, grads, *live_total = refs[9 + n_alias : 15 + n_alias + (rider > 0)]
    bias, weight, live, ks, vs, qs, cs, dka, dva = refs[15 + n_alias + (rider > 0) :]
    stride = OWN + rider

    @pl.when(pl.program_id(0) == 0)
    def _():
        key = lax.broadcasted_iota(jnp.int32, (SLOTS, PREFIX), 1)
        row = lax.broadcasted_iota(jnp.int32, (SLOTS, SLOTS), 0)
        col = lax.broadcasted_iota(jnp.int32, (SLOTS, SLOTS), 1)
        resp_bias = jnp.where(col <= row, 0.0, -jnp.inf)
        bias[:, :SLOTS] = resp_bias
        bias[:, SLOTS:KEYS] = jnp.where(key < prompt_len[0], 0.0, -jnp.inf)
        bias[:, KEYS:] = resp_bias
        mean = rewards[0, 0]
        for i in range(1, SPREAD):
            mean = mean + rewards[0, i]
        mean = mean * (1.0 / SPREAD)
        if rider:
            total = jnp.zeros((rider, HEAD_DIM), F32)
            for d in range(SPREAD):
                total = total + kv_ref[d * stride + OWN : (d + 1) * stride, :HEAD_DIM].astype(F32)
            live_total[0][...] = jnp.full((8, HEAD_DIM), jnp.sum(total), F32)
        for b in range(2):
            device = place[0] if b == 0 else place[0] + 1 - 2 * place[1]
            length = 0
            advantage = 0.0
            for i in range(SPREAD):
                here = resp_assign[0, i] == device
                length = length + jnp.where(here, resp_len[0, i], 0)
                advantage = advantage + jnp.where(here, rewards[0, i] - mean, 0.0)
            alive = jnp.where(row < length, 1.0, 0.0)
            live[b] = alive
            weight[b] = -advantage * alive
            if rider:
                weight[b] = -scale_of(live_total[0]) * (advantage * alive)

    ks[:SLOTS, :] = kr_ref[...]
    ks[KEYS:, :] = kr2_ref[...]
    vs[:SLOTS, :] = vr_ref[...]
    vs[KEYS:, :] = vr2_ref[...]
    for d in range(SPREAD):
        rows = slice(SLOTS + d * OWN, SLOTS + (d + 1) * OWN)
        ks[rows, :] = kv_ref[d * stride : d * stride + OWN, :HEAD_DIM]
        vs[rows, :] = kv_ref[d * stride : d * stride + OWN, HEAD_DIM:]
    for b, (q, do) in enumerate(((q_ref, do_ref), (q2_ref, do2_ref))):
        w = weight[b]
        for j in range(PER_KV):
            cols = slice(j * HEAD_DIM, (j + 1) * HEAD_DIM)
            rows = slice(j * SLOTS, (j + 1) * SLOTS)
            qs[b, rows, :] = q[:, cols]
            cs[b, rows, :] = (do[:, cols].astype(F32) * w).astype(BF)

    per = TILE // SLOTS
    tiles = PER_KV * SLOTS // TILE
    units = [(b, t) for b in range(2) for t in range(tiles)]
    spans = (slice(0, KEYS), slice(SLOTS, SLOTS + KEYS))

    def store(b, t, value, own, start):
        for i in range(per):
            j = t * per + i
            piece = value[i * SLOTS : (i + 1) * SLOTS]
            if b == 0:
                own[:, j * HEAD_DIM : (j + 1) * HEAD_DIM] = piece
            else:
                back[:, start + j * HEAD_DIM : start + (j + 1) * HEAD_DIM] = piece

    def softmax_part(b, t):
        rows = slice(t * TILE, (t + 1) * TILE)
        s = dot(qs[b, rows, :], ks[spans[b], :], NT)
        s = s + jnp.concatenate([bias[:, spans[b]]] * per, axis=0)
        m = jnp.max(s, axis=1, keepdims=True)
        p = jnp.exp2(s * SCALE2 - m * SCALE2)
        return p, 1.0 / jnp.sum(p, axis=1, keepdims=True)

    def score_part(b, t, p, inv):
        rows = slice(t * TILE, (t + 1) * TILE)
        c = cs[b, rows, :]
        att = p * inv
        ab = att.astype(BF)
        alive = jnp.concatenate([live[b]] * per, axis=0)
        ob = (dot(ab, vs[spans[b], :], NN) * alive).astype(BF)
        row_dot = jnp.sum(c.astype(F32) * ob.astype(F32), axis=1, keepdims=True)
        dp = dot(c, vs[spans[b], :], NT)
        ds = (att * (dp - row_dot)).astype(BF)
        store(b, t, ob, out_ref, 0)
        return ab, ds

    def grad_part(b, t, ab, ds):
        rows = slice(t * TILE, (t + 1) * TILE)
        store(b, t, (dot(ds, ks[spans[b], :], NN) * SCALE).astype(BF), dq_ref, WIDE)
        dv = dot(cs[b, rows, :].T, ab, NN)
        dk = dot(qs[b, rows, :].T, ds, NN)
        if t > 0:
            dv = dv + dva[b]
            dk = dk + dka[b]
        dva[b] = dv
        dka[b] = dk

    now = softmax_part(*units[0])
    last = None
    for u, unit in enumerate(units):
        later = softmax_part(*units[u + 1]) if u + 1 < len(units) else None
        if last is not None:
            grad_part(*units[u - 1], *last)
        last = score_part(*unit, *now)
        now = later
    grad_part(*units[-1], *last)

    dkr_ref[...] = (dka[0, :, :SLOTS] * SCALE).T.astype(BF)
    dvr_ref[...] = dva[0, :, :SLOTS].T.astype(BF)
    back[:, 2 * WIDE : 2 * WIDE + HEAD_DIM] = (dka[1, :, PREFIX:] * SCALE).T.astype(BF)
    back[:, 2 * WIDE + HEAD_DIM :] = dva[1, :, PREFIX:].T.astype(BF)
    grads[:, :HEAD_DIM] = ((dka[0, :, SLOTS:] + dka[1, :, :PREFIX]) * SCALE).T.astype(BF)
    grads[:, HEAD_DIM:] = (dva[0, :, SLOTS:] + dva[1, :, :PREFIX]).T.astype(BF)


def head_pass(scalars, arrays, others, kv, heads, bufs):
    mine = lambda g, place: (0, place[1] * LOCAL + heads[0] + g)
    at = lambda g, place: (0, g)
    wide = pl.BlockSpec((SLOTS, WIDE), mine)
    narrow = pl.BlockSpec((SLOTS, HEAD_DIM), mine)
    inputs = (*scalars, *arrays, *others, kv)
    n = len(heads)
    rider = kv.shape[0] // SPREAD - OWN
    extra = rider > 0
    return pl.pallas_call(
        functools.partial(head_kernel, len(bufs), rider),
        grid_spec=pltpu.PrefetchScalarGridSpec(
            num_scalar_prefetch=1,
            grid=(n,),
            in_specs=[SMEM] * 4
            + [wide, wide, narrow, narrow] * 2
            + [pl.BlockSpec((kv.shape[0], 2 * HEAD_DIM), at)]
            + [ANY] * len(bufs),
            out_specs=[
                wide,
                wide,
                narrow,
                narrow,
                pl.BlockSpec((SLOTS, PACK), at),
                pl.BlockSpec((PREFIX, 2 * HEAD_DIM), at),
            ]
            + [pl.BlockSpec((8, HEAD_DIM), lambda g, place: (0, 0))] * extra,
            scratch_shapes=[
                pltpu.VMEM((SLOTS, KEYS + SLOTS), F32),
                pltpu.VMEM((2, SLOTS, SLOTS), F32),
                pltpu.VMEM((2, SLOTS, SLOTS), F32),
                pltpu.VMEM((KEYS + SLOTS, HEAD_DIM), BF),
                pltpu.VMEM((KEYS + SLOTS, HEAD_DIM), BF),
                pltpu.VMEM((2, PER_KV * SLOTS, HEAD_DIM), BF),
                pltpu.VMEM((2, PER_KV * SLOTS, HEAD_DIM), BF),
                pltpu.VMEM((2, HEAD_DIM, KEYS), F32),
                pltpu.VMEM((2, HEAD_DIM, KEYS), F32),
            ],
        ),
        out_shape=[shape(SLOTS, HEADS * HEAD_DIM)] * 2
        + [shape(SLOTS, KV_HEADS * HEAD_DIM)] * 2
        + [shape(SLOTS, n * PACK), shape(PREFIX, n * 2 * HEAD_DIM)]
        + [shape(8, HEAD_DIM, dtype=F32)] * extra,
        input_output_aliases={len(inputs) + i: i for i in range(len(bufs))},
        compiler_params=pltpu.CompilerParams(vmem_limit_bytes=50 * 2**20),
        cost_estimate=pl.CostEstimate(
            flops=n * 12 * 2048 * KEYS * HEAD_DIM, bytes_accessed=n * 4 * 2**20, transcendentals=n * 2048 * KEYS
        ),
        name="head",
    )(*inputs, *bufs)


def tie(value, *others):
    return lax.optimization_barrier((value, *others))[0]


def body(
    queries, resp_keys, resp_values, prefix_keys, prefix_values, d_out, rewards, prompt_len, resp_len, resp_assign
):
    device = lax.axis_index("resp")
    place = jnp.stack([device, device % 2]).astype(jnp.int32)
    exchange = lambda x: lax.all_to_all(x, "resp", 0, 0, tiled=True)
    swap = lambda x: lax.ppermute(x, "resp", [(i, i ^ 1) for i in range(SPREAD)])
    spread = [(p * SPREAD + r, (p + r) % GROUPS * SPREAD + r) for p in range(GROUPS) for r in range(SPREAD)]
    lens = lax.ppermute(resp_len, ("prompt", "resp"), spread)

    arrays = (queries, d_out, resp_keys, resp_values)
    others = tuple(swap(x) for x in arrays)
    kv = exchange(pack_prompt(PARTS[0], prefix_keys, prefix_values))
    lens = jnp.pad(lens.astype(BF), ((0, RIDER - 1), (0, HEAD_DIM - SPREAD)))
    later, place = lax.optimization_barrier(
        (tie(pack_prompt(PARTS[1], prefix_keys, prefix_values, lens), kv, *others), place)
    )
    kv_later = exchange(later)

    scalars = (place, prompt_len, resp_len, resp_assign, rewards)
    *bufs, back, grads = head_pass(scalars, arrays, others, kv.reshape(PREFIX, -1), PARTS[0], [])
    terms = exchange(grads.reshape(SPREAD, OWN, -1))
    kv_later = kv_later.reshape(SPREAD * (OWN + RIDER), -1)
    *bufs, last_back, grads, total = head_pass(scalars, arrays, others, kv_later, PARTS[1], bufs)
    last_terms = exchange(tie(grads.reshape(SPREAD, OWN, -1), terms))

    sums = sum_terms(PARTS[0], True, total, terms)
    returned = swap(tie(back, *sums))
    last_returned = swap(tie(last_back, *sums))
    bufs = scale_rows(place, total, returned, PARTS[0], bufs)
    bufs = unpack_rows(place, last_returned, PARTS[1], bufs)
    *bufs, dk, dv = lax.optimization_barrier((*bufs, *sums))
    return (*bufs, *sum_terms(PARTS[1], False, last_terms, dk, dv))


def solution(mesh):
    rows = P(("prompt", "resp"), None)
    return jax.shard_map(
        body,
        mesh=mesh,
        in_specs=(rows,) * 6 + (P("prompt", None), P("prompt"), P("prompt", None), P("prompt", None)),
        out_specs=(rows,) * 6,
        check_vma=False,
    )
```

```python
import functools

import jax
import jax.numpy as jnp
from jax import lax
from jax.experimental import pallas as pl
from jax.experimental.pallas import tpu as pltpu
from jax.sharding import PartitionSpec as P

HEADS = 64
KV_HEADS = 8
HEAD_DIM = 128
PER_KV = HEADS // KV_HEADS
LOCAL = KV_HEADS // 2
SLOTS = 128
OWN = 64
PREFIX = 1024
LEAST = 512
KEYS = PREFIX + SLOTS
WIDE = PER_KV * HEAD_DIM
PACK = 2 * WIDE + 2 * HEAD_DIM
TILE = 512
SCALE = HEAD_DIM**-0.5
SCALE2 = SCALE * 1.4426950408889634
SPREAD = 16
GROUPS = 16
PARTS = ((0, 1), (2, 3))
RIDER = 16

BF = jnp.bfloat16
F32 = jnp.float32
NT = (((1,), (1,)), ((), ()))
NN = (((1,), (0,)), ((), ()))
ANY = pl.BlockSpec(memory_space=pl.ANY)
SMEM = pl.BlockSpec(memory_space=pltpu.SMEM)


def dot(a, b, dims):
    return lax.dot_general(a, b, dims, preferred_element_type=F32)


def shape(*dims, dtype=BF):
    return jax.ShapeDtypeStruct(dims, dtype)


def pack_prompt_kernel(heads, k_ref, v_ref, *refs):
    out = refs[-1]
    for n, h in enumerate(heads):
        for core in range(2):
            cols = slice((core * LOCAL + h) * HEAD_DIM, (core * LOCAL + h + 1) * HEAD_DIM)
            k = k_ref[:, cols]
            v = v_ref[:, cols]
            for chip in range(SPREAD // 2):
                out[2 * chip + core, :OWN, 2 * n * HEAD_DIM : (2 * n + 1) * HEAD_DIM] = k
                out[2 * chip + core, :OWN, (2 * n + 1) * HEAD_DIM : (2 * n + 2) * HEAD_DIM] = v
    if len(refs) > 1:
        lens = refs[0][...]
        for device in range(SPREAD):
            out[device, OWN:, :HEAD_DIM] = lens
            out[device, OWN:, HEAD_DIM:] = jnp.zeros((RIDER, (2 * len(heads) - 1) * HEAD_DIM), BF)


def pack_prompt(heads, keys, values, *lens):
    return pl.pallas_call(
        functools.partial(pack_prompt_kernel, heads),
        out_shape=shape(SPREAD, OWN + RIDER * len(lens), len(heads) * 2 * HEAD_DIM),
        name="pack_prompt",
    )(keys, values, *lens)


def scale_of(total):
    return jnp.full((1, HEAD_DIM), 1.0 * GROUPS * SPREAD * SLOTS, F32) / total[:1, :]


def unpack_rows_kernel(place, packed, *refs):
    out, dq, dk, dv = refs[-4:]
    out[...] = packed[:, :WIDE]
    dq[...] = packed[:, WIDE : 2 * WIDE]
    dk[...] = packed[:, 2 * WIDE : 2 * WIDE + HEAD_DIM]
    dv[...] = packed[:, 2 * WIDE + HEAD_DIM :]


def unpack_rows(place, packed, heads, bufs):
    theirs = lambda h, place: (0, (1 - place[1]) * LOCAL + heads[0] + h)
    wide = pl.BlockSpec((SLOTS, WIDE), theirs)
    narrow = pl.BlockSpec((SLOTS, HEAD_DIM), theirs)
    return pl.pallas_call(
        unpack_rows_kernel,
        grid_spec=pltpu.PrefetchScalarGridSpec(
            num_scalar_prefetch=1,
            grid=(len(heads),),
            in_specs=[pl.BlockSpec((SLOTS, PACK), lambda h, place: (0, h))] + [ANY] * 4,
            out_specs=[wide, wide, narrow, narrow],
        ),
        out_shape=[shape(SLOTS, HEADS * HEAD_DIM)] * 2 + [shape(SLOTS, KV_HEADS * HEAD_DIM)] * 2,
        input_output_aliases={2 + i: i for i in range(4)},
        name="unpack_rows",
    )(place, packed, *bufs)


def scale_rows_kernel(place, total, packed, dq_in, dk_in, dv_in, _, out, dq, dk, dv):
    scale = scale_of(total)

    def scaled(dst, src):
        for j in range(dst.shape[1] // HEAD_DIM):
            cols = slice(j * HEAD_DIM, (j + 1) * HEAD_DIM)
            dst[:, cols] = (src[:, cols].astype(F32) * scale).astype(BF)

    @pl.when(pl.program_id(1) == 0)
    def _():
        out[...] = packed[:, :WIDE]
        scaled(dq, packed.at[:, WIDE : 2 * WIDE])
        scaled(dk, packed.at[:, 2 * WIDE : 2 * WIDE + HEAD_DIM])
        scaled(dv, packed.at[:, 2 * WIDE + HEAD_DIM :])

    @pl.when(pl.program_id(1) == 1)
    def _():
        scaled(dq, dq_in)
        scaled(dk, dk_in)
        scaled(dv, dv_in)


def scale_rows(place, total, packed, heads, bufs):
    theirs = lambda h, side, place: (0, (1 - place[1]) * LOCAL + heads[0] + h)
    both = lambda h, side, place: (0, (1 - place[1] - side + 2 * side * place[1]) * LOCAL + heads[0] + h)
    wide = pl.BlockSpec((SLOTS, WIDE), both)
    narrow = pl.BlockSpec((SLOTS, HEAD_DIM), both)
    out, dq, dk, dv = bufs
    return pl.pallas_call(
        scale_rows_kernel,
        grid_spec=pltpu.PrefetchScalarGridSpec(
            num_scalar_prefetch=1,
            grid=(len(heads), 2),
            in_specs=[
                pl.BlockSpec((8, HEAD_DIM), lambda h, side, place: (0, 0)),
                pl.BlockSpec((SLOTS, PACK), lambda h, side, place: (0, h)),
                wide,
                narrow,
                narrow,
                ANY,
            ],
            out_specs=[pl.BlockSpec((SLOTS, WIDE), theirs), wide, narrow, narrow],
        ),
        out_shape=[shape(SLOTS, HEADS * HEAD_DIM)] * 2 + [shape(SLOTS, KV_HEADS * HEAD_DIM)] * 2,
        input_output_aliases={3: 1, 4: 2, 5: 3, 6: 0},
        name="scale_rows",
    )(place, total, packed, dq, dk, dv, out)


def sum_terms_kernel(heads, scaled, *refs):
    dk_ref, dv_ref = refs[-2:]
    if scaled:
        live_total, terms = refs[:2]
        scale = jnp.concatenate([scale_of(live_total)] * 2, axis=1)
    else:
        terms = refs[0]
        dk_ref[...] = refs[1][...]
        dv_ref[...] = refs[2][...]
    for n, h in enumerate(heads):
        cols = slice(2 * n * HEAD_DIM, (2 * n + 2) * HEAD_DIM)
        for core in range(2):
            total = terms[core, :, cols].astype(F32)
            for chip in range(1, SPREAD // 2):
                total = total + terms[2 * chip + core, :, cols].astype(F32)
            if scaled:
                total = total * scale
            total = total.astype(BF)
            own = slice((core * LOCAL + h) * HEAD_DIM, (core * LOCAL + h + 1) * HEAD_DIM)
            dk_ref[:, own] = total[:, :HEAD_DIM]
            dv_ref[:, own] = total[:, HEAD_DIM:]


def sum_terms(heads, scaled, *inputs):
    return pl.pallas_call(
        functools.partial(sum_terms_kernel, heads, scaled),
        out_shape=[shape(OWN, KV_HEADS * HEAD_DIM)] * 2,
        compiler_params=pltpu.CompilerParams(vmem_limit_bytes=16 * 2**20),
        name="sum_terms",
    )(*inputs)


def head_kernel(n_alias, rider, place, prompt_len, resp_len, resp_assign, rewards, *refs):
    q_ref, do_ref, kr_ref, vr_ref, q2_ref, do2_ref, kr2_ref, vr2_ref, kv_ref = refs[:9]
    out_ref, dq_ref, dkr_ref, dvr_ref, back, grads, *live_total = refs[9 + n_alias : 15 + n_alias + (rider > 0)]
    bias, weight, live, ks, vs, qs, cs, dka, dva = refs[15 + n_alias + (rider > 0) :]
    stride = OWN + rider

    @pl.when(pl.program_id(0) == 0)
    def _():
        key = lax.broadcasted_iota(jnp.int32, (SLOTS, PREFIX), 1)
        row = lax.broadcasted_iota(jnp.int32, (SLOTS, SLOTS), 0)
        col = lax.broadcasted_iota(jnp.int32, (SLOTS, SLOTS), 1)
        resp_bias = jnp.where(col <= row, 0.0, -jnp.inf)
        bias[:, :SLOTS] = resp_bias
        bias[:, SLOTS:KEYS] = jnp.where(key < prompt_len[0], 0.0, -jnp.inf)
        bias[:, KEYS:] = resp_bias
        mean = rewards[0, 0]
        for i in range(1, SPREAD):
            mean = mean + rewards[0, i]
        mean = mean * (1.0 / SPREAD)
        if rider:
            total = jnp.zeros((rider, HEAD_DIM), F32)
            for d in range(SPREAD):
                total = total + kv_ref[d * stride + OWN : (d + 1) * stride, :HEAD_DIM].astype(F32)
            live_total[0][...] = jnp.full((8, HEAD_DIM), jnp.sum(total), F32)
        for b in range(2):
            device = place[0] if b == 0 else place[0] + 1 - 2 * place[1]
            length = 0
            advantage = 0.0
            for i in range(SPREAD):
                here = resp_assign[0, i] == device
                length = length + jnp.where(here, resp_len[0, i], 0)
                advantage = advantage + jnp.where(here, rewards[0, i] - mean, 0.0)
            alive = jnp.where(row < length, 1.0, 0.0)
            live[b] = alive
            weight[b] = -advantage * alive
            if rider:
                weight[b] = -scale_of(live_total[0]) * (advantage * alive)

    ks[:SLOTS, :] = kr_ref[...]
    ks[KEYS:, :] = kr2_ref[...]
    vs[:SLOTS, :] = vr_ref[...]
    vs[KEYS:, :] = vr2_ref[...]
    for d in range(SPREAD):
        rows = slice(SLOTS + d * OWN, SLOTS + (d + 1) * OWN)
        ks[rows, :] = kv_ref[d * stride : d * stride + OWN, :HEAD_DIM]
        vs[rows, :] = kv_ref[d * stride : d * stride + OWN, HEAD_DIM:]
    for b, (q, do) in enumerate(((q_ref, do_ref), (q2_ref, do2_ref))):
        w = weight[b]
        for j in range(PER_KV):
            cols = slice(j * HEAD_DIM, (j + 1) * HEAD_DIM)
            rows = slice(j * SLOTS, (j + 1) * SLOTS)
            qs[b, rows, :] = q[:, cols]
            cs[b, rows, :] = (do[:, cols].astype(F32) * w).astype(BF)

    per = TILE // SLOTS
    tiles = PER_KV * SLOTS // TILE
    units = [(b, t) for b in range(2) for t in range(tiles)]
    spans = (slice(0, KEYS), slice(SLOTS, SLOTS + KEYS))

    def store(b, t, value, own, start):
        for i in range(per):
            j = t * per + i
            piece = value[i * SLOTS : (i + 1) * SLOTS]
            if b == 0:
                own[:, j * HEAD_DIM : (j + 1) * HEAD_DIM] = piece
            else:
                back[:, start + j * HEAD_DIM : start + (j + 1) * HEAD_DIM] = piece

    def softmax_part(b, t):
        rows = slice(t * TILE, (t + 1) * TILE)
        s = dot(qs[b, rows, :], ks[spans[b], :], NT)
        at = SLOTS if b == 0 else 0
        masked = [slice(0, at), slice(at + LEAST, KEYS)]
        pieces = [s[:, m] + jnp.concatenate([bias[:, spans[b]][:, m]] * per, axis=0) for m in masked if m.stop > 0]
        s = jnp.concatenate([*pieces[:-1], s[:, at : at + LEAST], pieces[-1]], axis=1)
        m = jnp.max(s, axis=1, keepdims=True)
        p = jnp.exp2(s * SCALE2 - m * SCALE2)
        return p, 1.0 / jnp.sum(p, axis=1, keepdims=True)

    def score_part(b, t, p, inv):
        rows = slice(t * TILE, (t + 1) * TILE)
        c = cs[b, rows, :]
        att = p * inv
        ab = att.astype(BF)
        alive = jnp.concatenate([live[b]] * per, axis=0)
        ob = (dot(ab, vs[spans[b], :], NN) * alive).astype(BF)
        row_dot = jnp.sum(c.astype(F32) * ob.astype(F32), axis=1, keepdims=True)
        dp = dot(c, vs[spans[b], :], NT)
        ds = (att * (dp - row_dot)).astype(BF)
        store(b, t, ob, out_ref, 0)
        return ab, ds

    def grad_part(b, t, ab, ds):
        rows = slice(t * TILE, (t + 1) * TILE)
        store(b, t, (dot(ds, ks[spans[b], :], NN) * SCALE).astype(BF), dq_ref, WIDE)
        dv = dot(cs[b, rows, :].T, ab, NN)
        dk = dot(qs[b, rows, :].T, ds, NN)
        if t > 0:
            dv = dv + dva[b]
            dk = dk + dka[b]
        dva[b] = dv
        dka[b] = dk

    now = softmax_part(*units[0])
    last = None
    for u, unit in enumerate(units):
        later = softmax_part(*units[u + 1]) if u + 1 < len(units) else None
        if last is not None:
            grad_part(*units[u - 1], *last)
        last = score_part(*unit, *now)
        now = later
    grad_part(*units[-1], *last)

    dkr_ref[...] = (dka[0, :, :SLOTS] * SCALE).astype(BF).T
    dvr_ref[...] = dva[0, :, :SLOTS].astype(BF).T
    back[:, 2 * WIDE : 2 * WIDE + HEAD_DIM] = (dka[1, :, PREFIX:] * SCALE).astype(BF).T
    back[:, 2 * WIDE + HEAD_DIM :] = dva[1, :, PREFIX:].astype(BF).T
    grads[:, :HEAD_DIM] = ((dka[0, :, SLOTS:] + dka[1, :, :PREFIX]) * SCALE).astype(BF).T
    grads[:, HEAD_DIM:] = (dva[0, :, SLOTS:] + dva[1, :, :PREFIX]).astype(BF).T


def head_pass(scalars, arrays, others, kv, heads, bufs):
    mine = lambda g, place: (0, place[1] * LOCAL + heads[0] + g)
    at = lambda g, place: (0, g)
    wide = pl.BlockSpec((SLOTS, WIDE), mine)
    narrow = pl.BlockSpec((SLOTS, HEAD_DIM), mine)
    inputs = (*scalars, *arrays, *others, kv)
    n = len(heads)
    rider = kv.shape[0] // SPREAD - OWN
    extra = rider > 0
    return pl.pallas_call(
        functools.partial(head_kernel, len(bufs), rider),
        grid_spec=pltpu.PrefetchScalarGridSpec(
            num_scalar_prefetch=1,
            grid=(n,),
            in_specs=[SMEM] * 4
            + [wide, wide, narrow, narrow] * 2
            + [pl.BlockSpec((kv.shape[0], 2 * HEAD_DIM), at)]
            + [ANY] * len(bufs),
            out_specs=[
                wide,
                wide,
                narrow,
                narrow,
                pl.BlockSpec((SLOTS, PACK), at),
                pl.BlockSpec((PREFIX, 2 * HEAD_DIM), at),
            ]
            + [pl.BlockSpec((8, HEAD_DIM), lambda g, place: (0, 0))] * extra,
            scratch_shapes=[
                pltpu.VMEM((SLOTS, KEYS + SLOTS), F32),
                pltpu.VMEM((2, SLOTS, SLOTS), F32),
                pltpu.VMEM((2, SLOTS, SLOTS), F32),
                pltpu.VMEM((KEYS + SLOTS, HEAD_DIM), BF),
                pltpu.VMEM((KEYS + SLOTS, HEAD_DIM), BF),
                pltpu.VMEM((2, PER_KV * SLOTS, HEAD_DIM), BF),
                pltpu.VMEM((2, PER_KV * SLOTS, HEAD_DIM), BF),
                pltpu.VMEM((2, HEAD_DIM, KEYS), F32),
                pltpu.VMEM((2, HEAD_DIM, KEYS), F32),
            ],
        ),
        out_shape=[shape(SLOTS, HEADS * HEAD_DIM)] * 2
        + [shape(SLOTS, KV_HEADS * HEAD_DIM)] * 2
        + [shape(SLOTS, n * PACK), shape(PREFIX, n * 2 * HEAD_DIM)]
        + [shape(8, HEAD_DIM, dtype=F32)] * extra,
        input_output_aliases={len(inputs) + i: i for i in range(len(bufs))},
        compiler_params=pltpu.CompilerParams(vmem_limit_bytes=50 * 2**20),
        cost_estimate=pl.CostEstimate(
            flops=n * 12 * 2048 * KEYS * HEAD_DIM, bytes_accessed=n * 4 * 2**20, transcendentals=n * 2048 * KEYS
        ),
        name="head",
    )(*inputs, *bufs)


def tie(value, *others):
    return lax.optimization_barrier((value, *others))[0]


def body(
    queries, resp_keys, resp_values, prefix_keys, prefix_values, d_out, rewards, prompt_len, resp_len, resp_assign
):
    device = lax.axis_index("resp")
    place = jnp.stack([device, device % 2]).astype(jnp.int32)
    exchange = lambda x: lax.all_to_all(x, "resp", 0, 0, tiled=True)
    swap = lambda x: lax.ppermute(x, "resp", [(i, i ^ 1) for i in range(SPREAD)])
    spread = [(p * SPREAD + r, (p + r) % GROUPS * SPREAD + r) for p in range(GROUPS) for r in range(SPREAD)]
    lens = lax.ppermute(resp_len, ("prompt", "resp"), spread)

    arrays = (queries, d_out, resp_keys, resp_values)
    others = tuple(swap(x) for x in arrays)
    kv = exchange(pack_prompt(PARTS[0], prefix_keys, prefix_values))
    lens = jnp.pad(lens.astype(BF), ((0, RIDER - 1), (0, HEAD_DIM - SPREAD)))
    later, place = lax.optimization_barrier(
        (tie(pack_prompt(PARTS[1], prefix_keys, prefix_values, lens), kv, *others), place)
    )
    kv_later = exchange(later)

    scalars = (place, prompt_len, resp_len, resp_assign, rewards)
    *bufs, back, grads = head_pass(scalars, arrays, others, kv.reshape(PREFIX, -1), PARTS[0], [])
    terms = exchange(grads.reshape(SPREAD, OWN, -1))
    kv_later = kv_later.reshape(SPREAD * (OWN + RIDER), -1)
    *bufs, last_back, grads, total = head_pass(scalars, arrays, others, kv_later, PARTS[1], bufs)
    last_terms = exchange(tie(grads.reshape(SPREAD, OWN, -1), terms))

    sums = sum_terms(PARTS[0], True, total, terms)
    returned = swap(tie(back, *sums))
    last_returned = swap(tie(last_back, *sums))
    bufs = scale_rows(place, total, returned, PARTS[0], bufs)
    bufs = unpack_rows(place, last_returned, PARTS[1], bufs)
    *bufs, dk, dv = lax.optimization_barrier((*bufs, *sums))
    return (*bufs, *sum_terms(PARTS[1], False, last_terms, dk, dv))


def solution(mesh):
    rows = P(("prompt", "resp"), None)
    return jax.shard_map(
        body,
        mesh=mesh,
        in_specs=(rows,) * 6 + (P("prompt", None), P("prompt"), P("prompt", None), P("prompt", None)),
        out_specs=(rows,) * 6,
        check_vma=False,
    )
```

```python
import functools

import jax
import jax.numpy as jnp
from jax import lax
from jax.experimental import pallas as pl
from jax.experimental.pallas import tpu as pltpu
from jax.sharding import PartitionSpec as P

HEADS = 64
KV_HEADS = 8
HEAD_DIM = 128
PER_KV = HEADS // KV_HEADS
LOCAL = KV_HEADS // 2
SLOTS = 128
OWN = 64
PREFIX = 1024
LEAST = 512
KEYS = PREFIX + SLOTS
WIDE = PER_KV * HEAD_DIM
PACK = 2 * WIDE + 2 * HEAD_DIM
TILE = 512
SCALE = HEAD_DIM**-0.5
SCALE2 = SCALE * 1.4426950408889634
SPREAD = 16
GROUPS = 16
PARTS = ((0, 1), (2, 3))
RIDER = 16

BF = jnp.bfloat16
F32 = jnp.float32
NT = (((1,), (1,)), ((), ()))
NN = (((1,), (0,)), ((), ()))
SMALL = pl.CostEstimate(flops=1, bytes_accessed=1, transcendentals=0)
ANY = pl.BlockSpec(memory_space=pl.ANY)
SMEM = pl.BlockSpec(memory_space=pltpu.SMEM)


def dot(a, b, dims):
    return lax.dot_general(a, b, dims, preferred_element_type=F32)


def shape(*dims, dtype=BF):
    return jax.ShapeDtypeStruct(dims, dtype)


def pack_prompt_kernel(heads, k_ref, v_ref, *refs):
    out = refs[-1]
    for n, h in enumerate(heads):
        for core in range(2):
            cols = slice((core * LOCAL + h) * HEAD_DIM, (core * LOCAL + h + 1) * HEAD_DIM)
            k = k_ref[:, cols]
            v = v_ref[:, cols]
            for chip in range(SPREAD // 2):
                out[2 * chip + core, :OWN, 2 * n * HEAD_DIM : (2 * n + 1) * HEAD_DIM] = k
                out[2 * chip + core, :OWN, (2 * n + 1) * HEAD_DIM : (2 * n + 2) * HEAD_DIM] = v
    if len(refs) > 1:
        lens = refs[0][...]
        for device in range(SPREAD):
            out[device, OWN:, :HEAD_DIM] = lens
            out[device, OWN:, HEAD_DIM:] = jnp.zeros((RIDER, (2 * len(heads) - 1) * HEAD_DIM), BF)


def pack_prompt(heads, keys, values, *lens):
    return pl.pallas_call(
        functools.partial(pack_prompt_kernel, heads),
        out_shape=shape(SPREAD, OWN + RIDER * len(lens), len(heads) * 2 * HEAD_DIM),
        name="pack_prompt",
    )(keys, values, *lens)


def scale_of(total):
    return jnp.full((1, HEAD_DIM), 1.0 * GROUPS * SPREAD * SLOTS, F32) / total[:1, :]


def unpack_rows_kernel(place, packed, *refs):
    out, dq, dk, dv = refs[-4:]
    out[...] = packed[:, :WIDE]
    dq[...] = packed[:, WIDE : 2 * WIDE]
    dk[...] = packed[:, 2 * WIDE : 2 * WIDE + HEAD_DIM]
    dv[...] = packed[:, 2 * WIDE + HEAD_DIM :]


def unpack_rows(place, packed, heads, bufs):
    theirs = lambda h, place: (0, (1 - place[1]) * LOCAL + heads[0] + h)
    wide = pl.BlockSpec((SLOTS, WIDE), theirs)
    narrow = pl.BlockSpec((SLOTS, HEAD_DIM), theirs)
    return pl.pallas_call(
        unpack_rows_kernel,
        grid_spec=pltpu.PrefetchScalarGridSpec(
            num_scalar_prefetch=1,
            grid=(len(heads),),
            in_specs=[pl.BlockSpec((SLOTS, PACK), lambda h, place: (0, h))] + [ANY] * 4,
            out_specs=[wide, wide, narrow, narrow],
        ),
        out_shape=[shape(SLOTS, HEADS * HEAD_DIM)] * 2 + [shape(SLOTS, KV_HEADS * HEAD_DIM)] * 2,
        input_output_aliases={2 + i: i for i in range(4)},
        cost_estimate=SMALL,
        name="unpack_rows",
    )(place, packed, *bufs)


def scale_rows_kernel(place, total, packed, dq_in, dk_in, dv_in, _, out, dq, dk, dv):
    scale = scale_of(total)

    def scaled(dst, src):
        for j in range(dst.shape[1] // HEAD_DIM):
            cols = slice(j * HEAD_DIM, (j + 1) * HEAD_DIM)
            dst[:, cols] = (src[:, cols].astype(F32) * scale).astype(BF)

    @pl.when(pl.program_id(1) == 0)
    def _():
        out[...] = packed[:, :WIDE]
        scaled(dq, packed.at[:, WIDE : 2 * WIDE])
        scaled(dk, packed.at[:, 2 * WIDE : 2 * WIDE + HEAD_DIM])
        scaled(dv, packed.at[:, 2 * WIDE + HEAD_DIM :])

    @pl.when(pl.program_id(1) == 1)
    def _():
        scaled(dq, dq_in)
        scaled(dk, dk_in)
        scaled(dv, dv_in)


def scale_rows(place, total, packed, heads, bufs):
    theirs = lambda h, side, place: (0, (1 - place[1]) * LOCAL + heads[0] + h)
    both = lambda h, side, place: (0, (1 - place[1] - side + 2 * side * place[1]) * LOCAL + heads[0] + h)
    wide = pl.BlockSpec((SLOTS, WIDE), both)
    narrow = pl.BlockSpec((SLOTS, HEAD_DIM), both)
    out, dq, dk, dv = bufs
    return pl.pallas_call(
        scale_rows_kernel,
        grid_spec=pltpu.PrefetchScalarGridSpec(
            num_scalar_prefetch=1,
            grid=(len(heads), 2),
            in_specs=[
                pl.BlockSpec((8, HEAD_DIM), lambda h, side, place: (0, 0)),
                pl.BlockSpec((SLOTS, PACK), lambda h, side, place: (0, h)),
                wide,
                narrow,
                narrow,
                ANY,
            ],
            out_specs=[pl.BlockSpec((SLOTS, WIDE), theirs), wide, narrow, narrow],
        ),
        out_shape=[shape(SLOTS, HEADS * HEAD_DIM)] * 2 + [shape(SLOTS, KV_HEADS * HEAD_DIM)] * 2,
        input_output_aliases={3: 1, 4: 2, 5: 3, 6: 0},
        cost_estimate=SMALL,
        name="scale_rows",
    )(place, total, packed, dq, dk, dv, out)


def sum_terms_kernel(heads, scaled, *refs):
    dk_ref, dv_ref = refs[-2:]
    if scaled:
        live_total, terms = refs[:2]
        scale = jnp.concatenate([scale_of(live_total)] * 2, axis=1)
    else:
        terms = refs[0]
        dk_ref[...] = refs[1][...]
        dv_ref[...] = refs[2][...]
    for n, h in enumerate(heads):
        cols = slice(2 * n * HEAD_DIM, (2 * n + 2) * HEAD_DIM)
        for core in range(2):
            total = terms[core, :, cols].astype(F32)
            for chip in range(1, SPREAD // 2):
                total = total + terms[2 * chip + core, :, cols].astype(F32)
            if scaled:
                total = total * scale
            total = total.astype(BF)
            own = slice((core * LOCAL + h) * HEAD_DIM, (core * LOCAL + h + 1) * HEAD_DIM)
            dk_ref[:, own] = total[:, :HEAD_DIM]
            dv_ref[:, own] = total[:, HEAD_DIM:]


def sum_terms(heads, scaled, *inputs):
    return pl.pallas_call(
        functools.partial(sum_terms_kernel, heads, scaled),
        out_shape=[shape(OWN, KV_HEADS * HEAD_DIM)] * 2,
        compiler_params=pltpu.CompilerParams(vmem_limit_bytes=16 * 2**20),
        cost_estimate=SMALL,
        name="sum_terms",
    )(*inputs)


def head_kernel(n_alias, rider, place, resp_len, resp_assign, rewards, *refs):
    q_ref, do_ref, kr_ref, vr_ref, q2_ref, do2_ref, kr2_ref, vr2_ref, kv_ref = refs[:9]
    out_ref, dq_ref, dkr_ref, dvr_ref, back, grads, *live_total = refs[9 + n_alias : 15 + n_alias + (rider > 0)]
    bias, weight, live, ks, vs, qs, cs, dka, dva = refs[15 + n_alias + (rider > 0) :]
    stride = OWN + rider

    @pl.when(pl.program_id(0) == 0)
    def _():
        key = lax.broadcasted_iota(jnp.int32, (SLOTS, PREFIX), 1)
        row = lax.broadcasted_iota(jnp.int32, (SLOTS, SLOTS), 0)
        col = lax.broadcasted_iota(jnp.int32, (SLOTS, SLOTS), 1)
        resp_bias = jnp.where(col <= row, 0.0, -jnp.inf)
        bias[:, :SLOTS] = resp_bias
        bias[:, SLOTS:KEYS] = jnp.where(key < place[2], 0.0, -jnp.inf)
        bias[:, KEYS:] = resp_bias
        mean = rewards[0, 0]
        for i in range(1, SPREAD):
            mean = mean + rewards[0, i]
        mean = mean * (1.0 / SPREAD)
        if rider:
            total = jnp.zeros((rider, HEAD_DIM), F32)
            for d in range(SPREAD):
                total = total + kv_ref[d * stride + OWN : (d + 1) * stride, :HEAD_DIM].astype(F32)
            live_total[0][...] = jnp.full((8, HEAD_DIM), jnp.sum(total), F32)
        for b in range(2):
            device = place[0] if b == 0 else place[0] + 1 - 2 * place[1]
            length = 0
            advantage = 0.0
            for i in range(SPREAD):
                here = resp_assign[0, i] == device
                length = length + jnp.where(here, resp_len[0, i], 0)
                advantage = advantage + jnp.where(here, rewards[0, i] - mean, 0.0)
            alive = jnp.where(row < length, 1.0, 0.0)
            live[b] = alive
            weight[b] = -advantage * alive
            if rider:
                weight[b] = -scale_of(live_total[0]) * (advantage * alive)

    ks[:SLOTS, :] = kr_ref[...]
    ks[KEYS:, :] = kr2_ref[...]
    vs[:SLOTS, :] = vr_ref[...]
    vs[KEYS:, :] = vr2_ref[...]
    for d in range(SPREAD):
        rows = slice(SLOTS + d * OWN, SLOTS + (d + 1) * OWN)
        ks[rows, :] = kv_ref[d * stride : d * stride + OWN, :HEAD_DIM]
        vs[rows, :] = kv_ref[d * stride : d * stride + OWN, HEAD_DIM:]
    for b, (q, do) in enumerate(((q_ref, do_ref), (q2_ref, do2_ref))):
        w = weight[b]
        for j in range(PER_KV):
            cols = slice(j * HEAD_DIM, (j + 1) * HEAD_DIM)
            rows = slice(j * SLOTS, (j + 1) * SLOTS)
            qs[b, rows, :] = q[:, cols]
            cs[b, rows, :] = (do[:, cols].astype(F32) * w).astype(BF)

    per = TILE // SLOTS
    tiles = PER_KV * SLOTS // TILE
    units = [(b, t) for b in range(2) for t in range(tiles)]
    spans = (slice(0, KEYS), slice(SLOTS, SLOTS + KEYS))

    def store(b, t, value, own, start):
        for i in range(per):
            j = t * per + i
            piece = value[i * SLOTS : (i + 1) * SLOTS]
            if b == 0:
                own[:, j * HEAD_DIM : (j + 1) * HEAD_DIM] = piece
            else:
                back[:, start + j * HEAD_DIM : start + (j + 1) * HEAD_DIM] = piece

    def softmax_part(b, t):
        rows = slice(t * TILE, (t + 1) * TILE)
        s = dot(qs[b, rows, :], ks[spans[b], :], NT)
        at = SLOTS if b == 0 else 0
        masked = [slice(0, at), slice(at + LEAST, KEYS)]
        pieces = [s[:, m] + jnp.concatenate([bias[:, spans[b]][:, m]] * per, axis=0) for m in masked if m.stop > 0]
        s = jnp.concatenate([*pieces[:-1], s[:, at : at + LEAST], pieces[-1]], axis=1)
        m = jnp.max(s, axis=1, keepdims=True)
        p = jnp.exp2(s * SCALE2 - m * SCALE2)
        return p, 1.0 / jnp.sum(p, axis=1, keepdims=True)

    def score_part(b, t, p, inv):
        rows = slice(t * TILE, (t + 1) * TILE)
        c = cs[b, rows, :]
        att = p * inv
        ab = att.astype(BF)
        alive = jnp.concatenate([live[b]] * per, axis=0)
        ob = (dot(ab, vs[spans[b], :], NN) * alive).astype(BF)
        row_dot = jnp.sum(c.astype(F32) * ob.astype(F32), axis=1, keepdims=True)
        dp = dot(c, vs[spans[b], :], NT)
        ds = (att * (dp - row_dot)).astype(BF)
        store(b, t, ob, out_ref, 0)
        return ab, ds

    def grad_part(b, t, ab, ds):
        rows = slice(t * TILE, (t + 1) * TILE)
        store(b, t, (dot(ds, ks[spans[b], :], NN) * SCALE).astype(BF), dq_ref, WIDE)
        dv = dot(cs[b, rows, :].T, ab, NN)
        dk = dot(qs[b, rows, :].T, ds, NN)
        if t > 0:
            dv = dv + dva[b]
            dk = dk + dka[b]
        dva[b] = dv
        dka[b] = dk

    now = softmax_part(*units[0])
    last = None
    for u, unit in enumerate(units):
        later = softmax_part(*units[u + 1]) if u + 1 < len(units) else None
        if last is not None:
            grad_part(*units[u - 1], *last)
        last = score_part(*unit, *now)
        now = later
    grad_part(*units[-1], *last)

    dkr_ref[...] = (dka[0, :, :SLOTS] * SCALE).astype(BF).T
    dvr_ref[...] = dva[0, :, :SLOTS].astype(BF).T
    back[:, 2 * WIDE : 2 * WIDE + HEAD_DIM] = (dka[1, :, PREFIX:] * SCALE).astype(BF).T
    back[:, 2 * WIDE + HEAD_DIM :] = dva[1, :, PREFIX:].astype(BF).T
    grads[:, :HEAD_DIM] = ((dka[0, :, SLOTS:] + dka[1, :, :PREFIX]) * SCALE).astype(BF).T
    grads[:, HEAD_DIM:] = (dva[0, :, SLOTS:] + dva[1, :, :PREFIX]).astype(BF).T


def head_pass(scalars, arrays, others, kv, heads, bufs):
    mine = lambda g, place: (0, place[1] * LOCAL + heads[0] + g)
    at = lambda g, place: (0, g)
    wide = pl.BlockSpec((SLOTS, WIDE), mine)
    narrow = pl.BlockSpec((SLOTS, HEAD_DIM), mine)
    inputs = (*scalars, *arrays, *others, kv)
    n = len(heads)
    rider = kv.shape[0] // SPREAD - OWN
    extra = rider > 0
    return pl.pallas_call(
        functools.partial(head_kernel, len(bufs), rider),
        grid_spec=pltpu.PrefetchScalarGridSpec(
            num_scalar_prefetch=1,
            grid=(n,),
            in_specs=[SMEM] * 3
            + [wide, wide, narrow, narrow] * 2
            + [pl.BlockSpec((kv.shape[0], 2 * HEAD_DIM), at)]
            + [ANY] * len(bufs),
            out_specs=[
                wide,
                wide,
                narrow,
                narrow,
                pl.BlockSpec((SLOTS, PACK), at),
                pl.BlockSpec((PREFIX, 2 * HEAD_DIM), at),
            ]
            + [pl.BlockSpec((8, HEAD_DIM), lambda g, place: (0, 0))] * extra,
            scratch_shapes=[
                pltpu.VMEM((SLOTS, KEYS + SLOTS), F32),
                pltpu.VMEM((2, SLOTS, SLOTS), F32),
                pltpu.VMEM((2, SLOTS, SLOTS), F32),
                pltpu.VMEM((KEYS + SLOTS, HEAD_DIM), BF),
                pltpu.VMEM((KEYS + SLOTS, HEAD_DIM), BF),
                pltpu.VMEM((2, PER_KV * SLOTS, HEAD_DIM), BF),
                pltpu.VMEM((2, PER_KV * SLOTS, HEAD_DIM), BF),
                pltpu.VMEM((2, HEAD_DIM, KEYS), F32),
                pltpu.VMEM((2, HEAD_DIM, KEYS), F32),
            ],
        ),
        out_shape=[shape(SLOTS, HEADS * HEAD_DIM)] * 2
        + [shape(SLOTS, KV_HEADS * HEAD_DIM)] * 2
        + [shape(SLOTS, n * PACK), shape(PREFIX, n * 2 * HEAD_DIM)]
        + [shape(8, HEAD_DIM, dtype=F32)] * extra,
        input_output_aliases={len(inputs) + i: i for i in range(len(bufs))},
        compiler_params=pltpu.CompilerParams(vmem_limit_bytes=50 * 2**20),
        cost_estimate=pl.CostEstimate(
            flops=n * 12 * 2048 * KEYS * HEAD_DIM, bytes_accessed=n * 4 * 2**20, transcendentals=n * 2048 * KEYS
        ),
        name="head",
    )(*inputs, *bufs)


def tie(value, *others):
    return lax.optimization_barrier((value, *others))[0]


def body(
    queries, resp_keys, resp_values, prefix_keys, prefix_values, d_out, rewards, prompt_len, resp_len, resp_assign
):
    device = lax.axis_index("resp")
    place = jnp.stack([device, device % 2, prompt_len[0]]).astype(jnp.int32)
    exchange = lambda x: lax.all_to_all(x, "resp", 0, 0, tiled=True)
    swap = lambda x: lax.ppermute(x, "resp", [(i, i ^ 1) for i in range(SPREAD)])
    spread = [(p * SPREAD + r, (p + r) % GROUPS * SPREAD + r) for p in range(GROUPS) for r in range(SPREAD)]
    lens = lax.ppermute(resp_len, ("prompt", "resp"), spread)

    arrays = (queries, d_out, resp_keys, resp_values)
    others = tuple(swap(x) for x in arrays)
    kv = exchange(pack_prompt(PARTS[0], prefix_keys, prefix_values))
    lens = jnp.pad(lens.astype(BF), ((0, RIDER - 1), (0, HEAD_DIM - SPREAD)))
    later, place = lax.optimization_barrier(
        (tie(pack_prompt(PARTS[1], prefix_keys, prefix_values, lens), kv, *others), place)
    )
    kv_later = exchange(later)

    scalars = (place, resp_len, resp_assign, rewards)
    *bufs, back, grads = head_pass(scalars, arrays, others, kv.reshape(PREFIX, -1), PARTS[0], [])
    terms = exchange(grads.reshape(SPREAD, OWN, -1))
    kv_later = kv_later.reshape(SPREAD * (OWN + RIDER), -1)
    *bufs, last_back, grads, total = head_pass(scalars, arrays, others, kv_later, PARTS[1], bufs)
    last_terms = exchange(tie(grads.reshape(SPREAD, OWN, -1), terms))

    sums = sum_terms(PARTS[0], True, total, terms)
    returned = swap(tie(back, *sums))
    last_returned = swap(tie(last_back, *sums))
    bufs = scale_rows(place, total, returned, PARTS[0], bufs)
    bufs = unpack_rows(place, last_returned, PARTS[1], bufs)
    *bufs, dk, dv = lax.optimization_barrier((*bufs, *sums))
    return (*bufs, *sum_terms(PARTS[1], False, last_terms, dk, dv))


def solution(mesh):
    rows = P(("prompt", "resp"), None)
    return jax.shard_map(
        body,
        mesh=mesh,
        in_specs=(rows,) * 6 + (P("prompt", None), P("prompt"), P("prompt", None), P("prompt", None)),
        out_specs=(rows,) * 6,
        check_vma=False,
    )
```
